256 devices in a mesh: frame: 16 (over y_lo, x, core), tok: 16 (over y_hi, z).
Axes of the slice: x: 4, y: 4 (y_hi: 2, y_lo: 2; y = y_hi * 2 + y_lo), z: 8, core: 2. Of those that a mesh axis runs over, the one named last changes fastest.
Arguments:
- inputs: bfloat16 [16, 2048, 4096], P('frame', 'tok'), may hold values from -40 to 40
- grad_attn: bfloat16 [16, 2048, 2048], P('frame', None, 'tok'), may hold values from -6 to 6
- w_qkv: bfloat16 [4096, 3, 2048], P(None, None, 'tok'), may hold values from -0.09375 to 0.09375
Outputs:
- grad_qkv: bfloat16 [4096, 3, 2048], P('frame', None, 'tok')
The draws below stay inside these ranges and needn't reach their ends.
All inputs are finite; a program needn't handle non-finite values.
Results may differ from the reference program's by a relative error of at most 0.009.
The reference program's roundings to bfloat16 on the way count: a program that leaves them out, or rounds other values in their place, can miss the bound.
Values may be sent and summed in bfloat16 or wider, within the bound.
No kernel may reach another device: no remote copies, remote signals or barrier semaphores. Data moves between devices by JAX's collectives and lax.ppermute only.
A program may use at most 128 MiB of HBM per device.

```python
import math
import jax
import jax.numpy as jnp
from jax import lax

D = 4096
HEADS = 16
HEAD_DIM = 128
ATTN = 2048
FRAMES = 16
PATCHES = 2048


def draw_inputs(key, part):
    key = jax.random.fold_in(key, 11)
    normal_key = jax.random.fold_in(key, 0)
    order_key = jax.random.fold_in(key, 2)
    values = jax.random.normal(normal_key, (FRAMES, PATCHES, D), jnp.float32)
    order = jax.random.permutation(order_key, FRAMES)
    blocks = jnp.arange(D) // (D // FRAMES)
    boosted = blocks[None, :] == order[:, None]
    values = values * jnp.where(boosted, 3.0, 1.0)[:, None, :]
    return jnp.clip(values, -40.0, 40.0).astype(jnp.bfloat16)


def block_scale(stream_key, shape, pieces, smallest, top_value):
    def one(dim, shards_of):
        steps = jax.random.uniform(jax.random.fold_in(jax.random.fold_in(stream_key, 6), dim), (shards_of,), jnp.float32, smallest / len(pieces), top_value / len(pieces))
        return jnp.repeat(jnp.exp(steps), shape[dim] // shards_of).reshape((-1,) + (1,) * (len(shape) - dim - 1))

    loudness = one(*pieces[0])
    for cut in pieces[1:]:
        loudness = loudness * one(*cut)
    return loudness


def centred(own_key, dims, scale, most, cuts=(), dtype=jnp.bfloat16):
    level = block_scale(own_key, dims, cuts, -0.22, 0.18) if cuts else 1.0
    drawn = jax.random.normal(own_key, dims, jnp.float32) * scale * level
    return jnp.minimum(jnp.maximum(drawn, -most), most).astype(dtype)


def setup_inputs(seed: int = 0) -> dict:
    keys = jax.random.split(jax.random.key(seed), 4)
    return {
        "inputs": draw_inputs(jax.random.fold_in(keys[3], 71), 0),
        "grad_attn": centred(keys[1], (FRAMES, PATCHES, ATTN), 1.0, 6.0, ((0, 16), (2, 16))),
        "w_qkv": centred(keys[2], (D, 3, ATTN), D ** -0.5, 0.09375, ((2, 16),)),
    }


def attend_probs(query_t, key_t):
    factor = 1.0 / math.sqrt(query_t.shape[-1])
    scores = jnp.einsum('tphd,sphd->phts', query_t.astype(jnp.float32), key_t.astype(jnp.float32)) * factor
    frame_count = scores.shape[-1]
    steps_idx = jnp.arange(frame_count)
    causal = steps_idx[None, :] <= steps_idx[:, None]
    scores = jnp.where(causal, scores, -1e+30)
    maxima = lax.optimization_barrier(jnp.max(scores, axis=-1, keepdims=True))
    exponent = jnp.exp(scores - maxima)
    return exponent / lax.optimization_barrier(jnp.sum(exponent, axis=-1, keepdims=True))

def attend_backward(query_t, key_t, value_t, attention, grad_t):
    factor = 1.0 / math.sqrt(query_t.shape[-1])
    grad_probs = jnp.einsum('tphd,sphd->phts', grad_t.astype(jnp.float32), value_t.astype(jnp.float32))
    row_dot = lax.optimization_barrier(jnp.sum(grad_probs * attention, axis=-1, keepdims=True))
    grad_scores = (attention * (grad_probs - row_dot)).astype(jnp.bfloat16).astype(jnp.float32)
    weights_b = attention.astype(jnp.bfloat16).astype(jnp.float32)
    grad_query = jnp.einsum('phts,sphd->tphd', grad_scores, key_t.astype(jnp.float32)) * factor
    grad_keys = jnp.einsum('phts,tphd->sphd', grad_scores, query_t.astype(jnp.float32)) * factor
    grad_values = jnp.einsum('phts,tphd->sphd', weights_b, grad_t.astype(jnp.float32))
    return (grad_query.astype(jnp.bfloat16), grad_keys.astype(jnp.bfloat16), grad_values.astype(jnp.bfloat16))

def reference(inputs, grad_attn, w_qkv):
    weights_f = w_qkv.astype(jnp.float32)

    def project(frame_in):
        return jnp.einsum('pd,djc->pjc', frame_in.astype(jnp.float32), weights_f).astype(jnp.bfloat16)
    projected = lax.map(project, inputs)
    projected = projected.reshape(FRAMES, PATCHES, 3, HEADS, HEAD_DIM)
    grad_heads = grad_attn.reshape(FRAMES, PATCHES, HEADS, HEAD_DIM)
    query_t = projected[:, :, 0]
    key_t = projected[:, :, 1]
    value_t = projected[:, :, 2]
    attention = attend_probs(query_t, key_t)
    grad_query, grad_keys, grad_values = attend_backward(query_t, key_t, value_t, attention, grad_heads)
    grad_proj = jnp.stack((grad_query, grad_keys, grad_values), axis=2).reshape(FRAMES, PATCHES, 3, HEADS * HEAD_DIM)

    def add_frame(total, items):
        frame_in, frame_grad = items
        term = jnp.einsum('pd,pjc->djc', frame_in.astype(jnp.float32), frame_grad.astype(jnp.float32))
        return (total + term, None)
    start_total = jnp.zeros((D, 3, HEADS * HEAD_DIM), jnp.float32)
    grad_qkv, _ = lax.scan(add_frame, start_total, (inputs, grad_proj))
    return grad_qkv.astype(jnp.bfloat16)
```

```python
import functools
import math

import jax
import jax.numpy as jnp
from jax import lax
from jax.experimental import pallas as pl
from jax.experimental.pallas import tpu as pltpu
from jax.sharding import Mesh, PartitionSpec as P

HEAD_DIM = 128
AXES = ("yl", "x", "core", "yh", "z")
SIZES = (2, 4, 2, 2, 8)
FRAME = AXES[:3]
TOK = AXES[3:]
FRAMES = 16
PATCHES = 128
WIDTH = 4096
COLS = 3 * HEAD_DIM
ROWS = FRAMES * PATCHES
GROUP = 16
STEP = 512

SAME_CORE = ((0, 0), (0, 1), (0, -1), (1, 0), (0, 2), (1, 1), (1, -1), (1, 2))
SLOTS = [(dy, dx, dc) for dy, dx in SAME_CORE for dc in (0, 1)]


def shift(value, axis, by):
    count = SIZES[AXES.index(axis)]
    return lax.ppermute(value, axis, [(i, (i + by) % count) for i in range(count)])


def transpose_mesh(value, place=lambda row, col: (col, row)):
    pairs = []
    for row in range(16):
        for col in range(16):
            to_row, to_col = place(row, col)
            pairs.append((row * 16 + col, to_row * 16 + to_col))
    return lax.ppermute(value, AXES, pairs)


def gather_frames(own):
    half = PATCHES // 2
    quarter = PATCHES // 4
    low, high = slice(0, half), slice(half, PATCHES)
    left = shift(own, "x", 1)
    right = shift(own, "x", -1)
    other = shift(own, "yl", 1)
    far_low = shift(left[low], "x", 1)
    far_high = shift(right[high], "x", -1)
    other_left_low = shift(left[low], "yl", 1)
    other_right_low = shift(right[low], "yl", 1)
    other_left_high = shift(other[high], "x", 1)
    other_right_high = shift(other[high], "x", -1)
    other_far_low = shift(far_low, "yl", 1)
    other_far_a = shift(other_left_high[:quarter], "x", 1)
    other_far_b = shift(other_right_high[quarter:], "x", -1)
    pieces = [
        (0, 0, own),
        (1, 0, right),
        (2, 0, left),
        (3, 0, other),
        (4, 0, far_low),
        (4, half, far_high),
        (5, 0, other_right_low),
        (5, half, other_right_high),
        (6, 0, other_left_low),
        (6, half, other_left_high),
        (7, 0, other_far_low),
        (7, half, other_far_a),
        (7, half + quarter, other_far_b),
    ]
    out = []
    for place, first, piece in pieces:
        out.append((2 * place, first, piece))
        out.append((2 * place + 1, first, shift(piece, "core", 1)))
    return out


def frame_ids():
    yl, x, core = (lax.axis_index(name) for name in FRAME)
    ids = []
    for dy, dx, dc in SLOTS:
        ids.append((((yl + dy) % 2) * 4 + (x + dx) % 4) * 2 + (core + dc) % 2)
    return jnp.stack(ids).astype(jnp.int32)


def visible(ids):
    frame = jnp.repeat(ids, GROUP)
    patch = jnp.tile(jnp.arange(GROUP, dtype=jnp.int32), FRAMES)
    allowed = (frame[None, :] <= frame[:, None]) & (patch[None, :] == patch[:, None])
    return allowed.astype(jnp.float32)


def attend(proj, grads, mask, out):
    factor = 1.0 / math.sqrt(HEAD_DIM)
    size = FRAMES * GROUP

    def body(step, carry):
        rows = pl.ds(pl.multiple_of(step * GROUP, GROUP), GROUP)
        part = proj[:, rows, :].reshape(size, COLS)
        query, key, value = (part[:, j * HEAD_DIM : (j + 1) * HEAD_DIM] for j in range(3))
        grad = grads[:, rows, :].reshape(size, HEAD_DIM)
        across = (((1,), (1,)), ((), ()))
        down = (((0,), (0,)), ((), ()))
        dot = functools.partial(lax.dot_general, preferred_element_type=jnp.float32)
        scores = dot(query, key, across) * factor
        scores = jnp.where(mask[...] > 0.5, scores, -1e30)
        exponent = jnp.exp(scores - jnp.max(scores, axis=-1, keepdims=True))
        probs = exponent / jnp.sum(exponent, axis=-1, keepdims=True)
        grad_probs = dot(grad, value, across)
        row_dot = jnp.sum(grad_probs * probs, axis=-1, keepdims=True)
        grad_scores = (probs * (grad_probs - row_dot)).astype(jnp.bfloat16)
        probs_b = probs.astype(jnp.bfloat16)
        grad_query = jnp.dot(grad_scores, key, preferred_element_type=jnp.float32) * factor
        grad_key = dot(grad_scores, query, down) * factor
        grad_value = dot(probs_b, grad, down)
        for j, result in enumerate((grad_query, grad_key, grad_value)):
            out[:, rows, j * HEAD_DIM : (j + 1) * HEAD_DIM] = result.astype(jnp.bfloat16).reshape(
                FRAMES, GROUP, HEAD_DIM
            )
        return carry

    lax.fori_loop(0, PATCHES // GROUP, body, 0)


def kernel(places, ids, mask, w_ref, g_ref, *refs):
    count = len(places)
    pieces, out = refs[:count], refs[count]
    tokens, proj, grads, grad_proj, turned, sems = refs[count + 1 :]
    copies = []
    for index, (slot, first, ref) in enumerate(zip(*zip(*places), pieces)):
        rows = ref.shape[0]
        copies.append(
            pltpu.make_async_copy(
                ref, tokens.at[slot, pl.ds(first, rows)], sems.at[index]
            )
        )
    for copy in copies:
        copy.start()
    for slot in range(FRAMES):
        grads[slot] = g_ref[ids[slot]]
    for copy in copies:
        copy.wait()

    def project(step, carry):
        two = pl.ds(step * 2, 2)
        rows = tokens[two].reshape(2 * PATCHES, WIDTH)
        value = jnp.dot(rows, w_ref[...], preferred_element_type=jnp.float32)
        proj[two] = value.astype(jnp.bfloat16).reshape(2, PATCHES, COLS)
        return carry

    lax.fori_loop(0, FRAMES // 2, project, 0)
    attend(proj, grads, mask, grad_proj)
    for slot in range(FRAMES):
        part = grad_proj[slot].astype(jnp.float32)
        turned[:, slot * PATCHES : (slot + 1) * PATCHES] = part.T.astype(jnp.bfloat16)

    def weigh(step, carry):
        columns = pl.ds(pl.multiple_of(step * STEP, STEP), STEP)
        rows = tokens[:, :, columns].reshape(ROWS, STEP)
        value = jnp.dot(turned[...], rows, preferred_element_type=jnp.float32)
        out[columns, :] = value.T.astype(jnp.bfloat16)
        return carry

    lax.fori_loop(0, WIDTH // STEP, weigh, 0)


def weight_share(pieces, ids, mask, w, g):
    places = [(slot, first) for slot, first, _ in pieces]
    vmem = pl.BlockSpec(memory_space=pltpu.VMEM)
    return pl.pallas_call(
        functools.partial(kernel, places),
        out_shape=jax.ShapeDtypeStruct((WIDTH, COLS), jnp.bfloat16),
        in_specs=[pl.BlockSpec(memory_space=pltpu.SMEM), vmem, vmem, vmem]
        + [pl.BlockSpec(memory_space=pl.ANY)] * len(pieces),
        out_specs=vmem,
        scratch_shapes=[
            pltpu.VMEM((FRAMES, PATCHES, WIDTH), jnp.bfloat16),
            pltpu.VMEM((FRAMES, PATCHES, COLS), jnp.bfloat16),
            pltpu.VMEM((FRAMES, PATCHES, HEAD_DIM), jnp.bfloat16),
            pltpu.VMEM((FRAMES, PATCHES, COLS), jnp.bfloat16),
            pltpu.VMEM((COLS, ROWS), jnp.bfloat16),
            pltpu.SemaphoreType.DMA((len(pieces),)),
        ],
        compiler_params=pltpu.CompilerParams(vmem_limit_bytes=56 * 2**20),
    )(ids, mask, w, g, *[piece for _, _, piece in pieces])


def local(inputs, grad_attn, w_qkv):
    frame = lax.axis_index(FRAME)
    yh = lax.axis_index("yh")
    start = (2 * (frame % 8) + frame // 8) * 256
    slice_w = lax.dynamic_slice_in_dim(w_qkv.reshape(WIDTH, COLS), start, 256, 0)
    slice_w = transpose_mesh(slice_w)
    swapped = shift(slice_w, "yh", 1)
    pair = jnp.where(
        yh == 0, jnp.concatenate((slice_w, swapped)), jnp.concatenate((swapped, slice_w))
    )
    w = lax.all_gather(pair, "z", axis=0, tiled=True)
    g = transpose_mesh(grad_attn[0]).reshape(FRAMES, PATCHES, HEAD_DIM)
    g = lax.all_to_all(g, TOK, split_axis=0, concat_axis=0, tiled=True)
    ids = frame_ids()
    mask = visible(ids)
    pieces = gather_frames(inputs[0])
    share = weight_share(pieces, ids, mask, w, g)
    mine = lax.psum_scatter(share, "z", scatter_dimension=0, tiled=True).reshape(2, 256, COLS)
    total = None
    for other in range(2):
        part = lax.dynamic_index_in_dim(mine, (yh + other) % 2, 0, keepdims=False)
        part = transpose_mesh(
            part, lambda row, col: (2 * (col % 8) + (col // 8 + other) % 2, row)
        ).astype(jnp.float32)
        total = part if total is None else total + part
    return total.astype(jnp.bfloat16).reshape(256, 3, HEAD_DIM)


def solution(mesh):
    fine = Mesh(mesh.devices.reshape(SIZES), AXES)
    in_specs = (P(FRAME, TOK, None), P(FRAME, None, TOK), P(None, None, TOK))
    out_specs = P(FRAME, None, TOK)
    return jax.shard_map(local, mesh=fine, in_specs=in_specs, out_specs=out_specs, check_vma=False)
```

```python
import functools
import math

import jax
import jax.numpy as jnp
import numpy as np
from jax import lax
from jax.experimental import pallas as pl
from jax.experimental.pallas import tpu as pltpu
from jax.sharding import Mesh, PartitionSpec as P

HEAD_DIM = 128
AXES = ("yl", "x", "core", "yh", "z")
SIZES = (2, 4, 2, 2, 8)
FRAME = AXES[:3]
TOK = AXES[3:]
FRAMES = 16
PATCHES = 128
HALF = PATCHES // 2
QUARTER = PATCHES // 4
WIDTH = 4096
COLS = 3 * HEAD_DIM
ROWS = FRAMES * PATCHES
GROUP = 16
CHUNK = WIDTH // 8

SAME_CORE = ((0, 0), (0, 1), (0, -1), (1, 0), (0, 2), (1, 1), (1, -1), (1, 2))
SLOTS = [(dy, dx, dc) for dy, dx in SAME_CORE for dc in (0, 1)]


def device(yl, x, core, yh, z):
    place = 0
    for value, size in zip((yl, x, core, yh, z), SIZES):
        place = place * size + value % size
    return place


def owner_moves(flip):
    pairs = []
    for yl in range(2):
        for x in range(4):
            for core in range(2):
                for yh in range(2):
                    for z in range(8):
                        source = device(yl, x, core, yh, z)
                        target = device(yl ^ (z // 4), x + z % 4, yh ^ flip, core, 4 * yl + x)
                        pairs.append((source, target))
    return pairs


def shift(value, axis, by):
    count = SIZES[AXES.index(axis)]
    return lax.ppermute(value, axis, [(i, (i + by) % count) for i in range(count)])


def gather_frames(own):
    join = lambda *parts: jnp.concatenate(parts, axis=0)
    left = shift(own, "x", 1)
    right = shift(own, "x", -1)
    other = shift(own, "yl", 1)
    twin = shift(own, "core", 1)
    from_left = shift(join(left[:HALF], other[HALF:]), "x", 1)
    from_right = shift(join(right[HALF:], other[HALF:]), "x", -1)
    from_other = shift(join(right[:HALF], left[:HALF]), "yl", 1)
    twin_a = shift(join(right, left, other), "core", 1)
    last_left = shift(from_left[HALF : HALF + QUARTER], "x", 1)
    last_right = shift(from_right[HALF + QUARTER :], "x", -1)
    last_other = shift(from_left[:HALF], "yl", 1)
    twin_b = shift(join(from_left, from_right, from_other), "core", 1)
    last = join(last_other, last_left, last_right)
    twin_c = shift(last, "core", 1)
    return (
        [own, twin, right, left, other, twin_a],
        [from_left, from_right, from_other, twin_b],
        [last, twin_c],
    )


FIRST = [
    [(0, 0, PATCHES)],
    [(1, 0, PATCHES)],
    [(2, 0, PATCHES)],
    [(4, 0, PATCHES)],
    [(6, 0, PATCHES)],
    [(3, 0, PATCHES), (5, 0, PATCHES), (7, 0, PATCHES)],
]


def second(core):
    return [
        [(8 + core, 0, HALF), (12 + core, HALF, HALF)],
        [(8 + core, HALF, HALF), (10 + core, HALF, HALF)],
        [(10 + core, 0, HALF), (12 + core, 0, HALF)],
    ]


SECOND = second(0) + [[part for buffer in second(1) for part in buffer]]
THIRD = [[(14, 0, PATCHES)], [(15, 0, PATCHES)]]


def parts_of(places):
    out = []
    for buffer, parts in enumerate(places):
        row = 0
        for slot, first, rows in parts:
            out.append((buffer, row // GROUP, slot, first // GROUP, rows // GROUP))
            row += rows
    return out


def tables():
    out = np.zeros((256, 48), np.int32)
    for yl, x, core, yh, z in np.ndindex(*SIZES):
        row = out[device(yl, x, core, yh, z)]
        for slot, (dy, dx, dc) in enumerate(SLOTS):
            row[slot] = (core ^ dc) * 8 + dy * 4 + dx % 4
            row[24 + slot] = ((yl ^ dy) * 4 + (x + dx) % 4) * 2 + (core ^ dc)
        for k in range(8):
            row[16 + k] = (yl ^ (k // 4)) * 4 + (x + k % 4) % 4
        row[40] = (yl ^ (z // 4)) * 4 + (x - z % 4) % 4
    return out


def visible(ids):
    frame = jnp.repeat(ids, GROUP)
    patch = jnp.tile(jnp.arange(GROUP, dtype=jnp.int32), FRAMES)
    allowed = (frame[None, :] <= frame[:, None]) & (patch[None, :] == patch[:, None])
    return allowed.astype(jnp.float32)


VMEM = pl.BlockSpec(memory_space=pltpu.VMEM)
SMEM = pl.BlockSpec(memory_space=pltpu.SMEM)
ANY = pl.BlockSpec(memory_space=pl.ANY)


def load_weights(w_ref, w, sem):
    copies = []
    for chunk in range(8):
        for j in range(3):
            copies.append(
                pltpu.make_async_copy(
                    w_ref.at[chunk, j],
                    w.at[pl.ds(chunk * CHUNK, CHUNK), pl.ds(j * HEAD_DIM, HEAD_DIM)],
                    sem.at[chunk * 3 + j],
                )
            )
    for copy in copies:
        copy.start()
    return copies


def project_rows(rows, w):
    return jnp.dot(rows, w[...], preferred_element_type=jnp.float32).astype(jnp.bfloat16)


def project_kernel(count, w_ref, *refs):
    buffers, out = refs[:count], refs[count]
    tokens, w, w_sem, sems = refs[count + 1 :]
    copies, at = [], 0
    for index, ref in enumerate(buffers):
        rows = ref.shape[0]
        copies.append(pltpu.make_async_copy(ref, tokens.at[pl.ds(at, rows)], sems.at[index]))
        at += rows
    loads = load_weights(w_ref, w, w_sem)
    for copy in copies:
        copy.start()
    for copy in loads + copies:
        copy.wait()
    block = 2 * PATCHES

    def body(step, carry):
        rows = pl.ds(pl.multiple_of(step * block, block), block)
        groups = pl.ds(step * (block // GROUP), block // GROUP)
        out[rows] = project_rows(tokens[groups].reshape(block, WIDTH), w)
        return carry

    lax.fori_loop(0, at * GROUP // block, body, 0)


def project(w, buffers):
    groups = sum(buffer.shape[0] for buffer in buffers)
    rows = groups * GROUP
    return pl.pallas_call(
        functools.partial(project_kernel, len(buffers)),
        out_shape=jax.ShapeDtypeStruct((rows, COLS), jnp.bfloat16),
        in_specs=[ANY] * (1 + len(buffers)),
        out_specs=VMEM,
        scratch_shapes=[
            pltpu.VMEM((groups, GROUP, WIDTH), jnp.bfloat16),
            pltpu.VMEM((WIDTH, COLS), jnp.bfloat16),
            pltpu.SemaphoreType.DMA((24,)),
            pltpu.SemaphoreType.DMA((len(buffers),)),
        ],
        compiler_params=pltpu.CompilerParams(vmem_limit_bytes=32 * 2**20),
        cost_estimate=pl.CostEstimate(
            flops=2 * rows * WIDTH * COLS, bytes_accessed=2 * (rows + COLS) * WIDTH, transcendentals=0
        ),
    )(w, *buffers)


def attend(proj, grads, mask, turned):
    factor = 1.0 / math.sqrt(HEAD_DIM)
    size = FRAMES * GROUP

    def body(step, carry):
        part = proj[step].reshape(size, COLS)
        query, key, value = (part[:, j * HEAD_DIM : (j + 1) * HEAD_DIM] for j in range(3))
        grad = grads[step].reshape(size, HEAD_DIM)
        across = (((1,), (1,)), ((), ()))
        down = (((0,), (0,)), ((), ()))
        dot = functools.partial(lax.dot_general, preferred_element_type=jnp.float32)
        scores = dot(query, key, across) * factor
        scores = jnp.where(mask[...] > 0.5, scores, -1e30)
        exponent = jnp.exp(scores - jnp.max(scores, axis=-1, keepdims=True))
        probs = exponent / jnp.sum(exponent, axis=-1, keepdims=True)
        grad_probs = dot(grad, value, across)
        row_dot = jnp.sum(grad_probs * probs, axis=-1, keepdims=True)
        grad_scores = (probs * (grad_probs - row_dot)).astype(jnp.bfloat16)
        probs_b = probs.astype(jnp.bfloat16)
        grad_query = jnp.dot(grad_scores, key, preferred_element_type=jnp.float32) * factor
        grad_key = dot(grad_scores, query, down) * factor
        grad_value = dot(probs_b, grad, down)
        columns = pl.ds(pl.multiple_of(step * size, size), size)
        for j, result in enumerate((grad_query, grad_key, grad_value)):
            turned[j * HEAD_DIM : (j + 1) * HEAD_DIM, columns] = result.T.astype(jnp.bfloat16)
        return carry

    lax.fori_loop(0, PATCHES // GROUP, body, 0)


def share_kernel(count, order, mask, w_ref, g_ref, proj_a, proj_b, *refs):
    buffers, out = refs[:count], refs[count]
    tokens, proj, grads, turned, w, shares, w_sem, x_sem, g_sem, p_sem, o_sem = refs[count + 1 :]
    token_copies = []
    for index, (buffer, at, slot, first, groups) in enumerate(parts_of(FIRST + SECOND + THIRD)):
        token_copies.append(
            pltpu.make_async_copy(
                buffers[buffer].at[pl.ds(at, groups)],
                tokens.at[pl.ds(first, groups), slot],
                x_sem.at[index],
            )
        )
    for copy in token_copies[-2:]:
        copy.start()
    loads = load_weights(w_ref, w, w_sem)
    small = []
    for slot in range(FRAMES):
        small.append(pltpu.make_async_copy(g_ref.at[order[slot]], grads.at[:, slot], g_sem.at[slot]))
    index = 0
    for source, places in ((proj_a, FIRST), (proj_b, SECOND)):
        at = 0
        for _, _, slot, first, groups in parts_of(places):
            small.append(
                pltpu.make_async_copy(
                    source.at[pl.ds(at, groups)],
                    proj.at[pl.ds(first, groups), slot],
                    p_sem.at[index],
                )
            )
            at += groups
            index += 1
    for copy in small + token_copies[:-2]:
        copy.start()
    for copy in token_copies[-2:] + loads:
        copy.wait()
    for slot in (14, 15):
        rows = project_rows(tokens[:, slot].reshape(PATCHES, WIDTH), w)
        proj[:, slot] = rows.reshape(PATCHES // GROUP, GROUP, COLS)
    for copy in small:
        copy.wait()
    attend(proj, grads, mask, turned)
    for copy in token_copies[:-2]:
        copy.wait()

    def weigh(step, carry):
        columns = pl.ds(pl.multiple_of(order[16 + step] * CHUNK, CHUNK), CHUNK)
        rows = tokens[:, :, :, columns].reshape(ROWS, CHUNK)
        value = jnp.dot(turned[...], rows, preferred_element_type=jnp.float32)
        for j in range(3):
            shares[step, j] = value[j * HEAD_DIM : (j + 1) * HEAD_DIM].T.astype(jnp.bfloat16)
        pltpu.make_async_copy(shares.at[step], out.at[step], o_sem.at[step]).start()
        return carry

    lax.fori_loop(0, 8, weigh, 0)
    for step in range(8):
        pltpu.make_async_copy(shares.at[step], out.at[step], o_sem.at[step]).wait()


def weight_share(order, mask, w, g, proj_a, proj_b, buffers):
    count = len(buffers)
    groups = PATCHES // GROUP
    token_parts = len(parts_of(FIRST + SECOND + THIRD))
    grouped = lambda value: value.reshape(-1, GROUP, COLS)
    return pl.pallas_call(
        functools.partial(share_kernel, count),
        out_shape=jax.ShapeDtypeStruct((8, 3, CHUNK, HEAD_DIM), jnp.bfloat16),
        in_specs=[SMEM, VMEM] + [ANY] * (4 + count),
        out_specs=ANY,
        scratch_shapes=[
            pltpu.VMEM((groups, FRAMES, GROUP, WIDTH), jnp.bfloat16),
            pltpu.VMEM((groups, FRAMES, GROUP, COLS), jnp.bfloat16),
            pltpu.VMEM((groups, FRAMES, GROUP, HEAD_DIM), jnp.bfloat16),
            pltpu.VMEM((COLS, ROWS), jnp.bfloat16),
            pltpu.VMEM((WIDTH, COLS), jnp.bfloat16),
            pltpu.VMEM((8, 3, CHUNK, HEAD_DIM), jnp.bfloat16),
            pltpu.SemaphoreType.DMA((24,)),
            pltpu.SemaphoreType.DMA((token_parts,)),
            pltpu.SemaphoreType.DMA((FRAMES,)),
            pltpu.SemaphoreType.DMA((token_parts - 2,)),
            pltpu.SemaphoreType.DMA((8,)),
        ],
        compiler_params=pltpu.CompilerParams(vmem_limit_bytes=44 * 2**20),
        cost_estimate=pl.CostEstimate(
            flops=2 * ROWS * WIDTH * COLS, bytes_accessed=2 * ROWS * WIDTH, transcendentals=0
        ),
    )(order, mask, w, g, grouped(proj_a), grouped(proj_b), *buffers)


def local(inputs, grad_attn, w_qkv):
    table = jnp.asarray(tables())[lax.axis_index(AXES)]
    to_worker = [(target, source) for source, target in owner_moves(0)]
    rows_w = lax.dynamic_slice(
        w_qkv.transpose(1, 0, 2), (0, table[40] * CHUNK, 0), (3, CHUNK, HEAD_DIM)
    )
    rows_w = lax.ppermute(rows_w.reshape(3 * CHUNK, HEAD_DIM), AXES, to_worker)
    w = lax.all_gather(rows_w, "z", axis=0, tiled=True).reshape(8, 3, CHUNK, HEAD_DIM)
    g = lax.ppermute(grad_attn[0], AXES, to_worker).reshape(FRAMES, PATCHES, HEAD_DIM)
    g = lax.all_to_all(g, TOK, split_axis=0, concat_axis=0, tiled=True)
    g = g.reshape(FRAMES, PATCHES // GROUP, GROUP, HEAD_DIM)
    steps = gather_frames(inputs[0])
    first, second_, third = (
        [buffer.reshape(-1, GROUP, WIDTH) for buffer in buffers] for buffers in steps
    )
    proj_a = project(w, first)
    proj_b = project(w, second_)
    share = weight_share(
        table[:24], visible(table[24:40]), w, g, proj_a, proj_b, first + second_ + third
    )
    mine = lax.psum_scatter(
        share.reshape(8 * 3 * CHUNK, HEAD_DIM), "z", scatter_dimension=0, tiled=True
    )
    mine = mine.reshape(3, 2, CHUNK // 2, HEAD_DIM)
    yh = lax.axis_index("yh")
    total = None
    for flip in range(2):
        part = lax.dynamic_index_in_dim(mine, (yh + flip) % 2, 1, keepdims=False)
        part = lax.ppermute(part, AXES, owner_moves(flip)).astype(jnp.float32)
        total = part if total is None else total + part
    return total.astype(jnp.bfloat16).transpose(1, 0, 2)


def solution(mesh):
    fine = Mesh(mesh.devices.reshape(SIZES), AXES)
    in_specs = (P(FRAME, TOK, None), P(FRAME, None, TOK), P(None, None, TOK))
    out_specs = P(FRAME, None, TOK)
    return jax.shard_map(local, mesh=fine, in_specs=in_specs, out_specs=out_specs, check_vma=False)
```

```python
import functools
import math

import jax
import jax.numpy as jnp
import numpy as np
from jax import lax
from jax.experimental import pallas as pl
from jax.experimental.pallas import tpu as pltpu
from jax.sharding import Mesh, PartitionSpec as P

HEAD_DIM = 128
AXES = ("yl", "x", "core", "yh", "z")
SIZES = (2, 4, 2, 2, 8)
FRAME = AXES[:3]
TOK = AXES[3:]
FRAMES = 16
PATCHES = 128
CUT_A, CUT_B = 48, 96
CUTS = ((0, CUT_A), (CUT_A, CUT_B), (CUT_B, PATCHES))
CUT_FLOPS = 3 * 10**10
WIDTH = 4096
COLS = 3 * HEAD_DIM
ROWS = FRAMES * PATCHES
GROUP = 16
CHUNK = WIDTH // 8

SAME_CORE = ((0, 0), (0, 1), (0, -1), (1, 0), (0, 2), (1, 1), (1, -1), (1, 2))
SLOTS = [(dy, dx, dc) for dy, dx in SAME_CORE for dc in (0, 1)]


def device(yl, x, core, yh, z):
    place = 0
    for value, size in zip((yl, x, core, yh, z), SIZES):
        place = place * size + value % size
    return place


def owner_moves(flip):
    pairs = []
    for yl in range(2):
        for x in range(4):
            for core in range(2):
                for yh in range(2):
                    for z in range(8):
                        source = device(yl, x, core, yh, z)
                        target = device(yl ^ (z % 2), x + z // 2, yh ^ flip, core, 2 * x + yl)
                        pairs.append((source, target))
    return pairs


def shift(value, axis, by):
    count = SIZES[AXES.index(axis)]
    return lax.ppermute(value, axis, [(i, (i + by) % count) for i in range(count)])


def after(values, *others):
    return lax.optimization_barrier((values, *others))[0]


def cut_kernel(*refs):
    sems = refs[-1]
    copies = []
    for index, (first, last) in enumerate(CUTS):
        source, target = refs[index], refs[3 + index]
        copies.append(
            pltpu.make_async_copy(source.at[pl.ds(first, last - first)], target, sems.at[index])
        )
        copies[-1].start()
    for copy in copies:
        copy.wait()


def cut(*buffers):
    hbm = pl.BlockSpec(memory_space=pltpu.HBM)
    return pl.pallas_call(
        cut_kernel,
        out_shape=[
            jax.ShapeDtypeStruct((last - first, WIDTH), jnp.bfloat16) for first, last in CUTS
        ],
        in_specs=[hbm] * 3,
        out_specs=[hbm] * 3,
        scratch_shapes=[pltpu.SemaphoreType.DMA((3,))],
        cost_estimate=pl.CostEstimate(flops=CUT_FLOPS, bytes_accessed=0, transcendentals=0),
    )(*buffers)


def gather_frames(own, early, middle):
    twin = lambda values: [shift(value, "core", 1) for value in values]
    first = [shift(own, "x", 1), shift(own, "x", -1), shift(own, "yl", 1)]
    own_twin = shift(own, "core", 1)
    left, right, other = after(first, *early)
    second = [shift(other, "x", 1), shift(right, "x", -1), shift(right, "yl", 1)]
    first_twins = twin([left, right, other])
    other_left, far, other_right = after(second, *middle)
    cuts = cut(other_left, other_right, far)
    third = [shift(cuts[0], "x", 1), shift(cuts[1], "x", -1), shift(cuts[2], "yl", 1)]
    second_twins = twin([other_left, far, other_right])
    third = after(third)
    return (
        [own, own_twin, left, right, other, *first_twins],
        [other_left, far, other_right, *second_twins],
        [*third, *twin(third)],
    )


FIRST = [[(slot, 0, PATCHES)] for slot in (0, 1, 4, 2, 6, 5, 3, 7)]
SECOND = [[(slot, 0, PATCHES)] for slot in (12, 8, 10, 13, 9, 11)]
THIRD = [
    [(14 + core, first, last - first)]
    for core in (0, 1)
    for first, last in CUTS
]


def parts_of(places):
    out = []
    for buffer, parts in enumerate(places):
        row = 0
        for slot, first, rows in parts:
            out.append((buffer, row // GROUP, slot, first // GROUP, rows // GROUP))
            row += rows
    return out


def tables():
    out = np.zeros((256, 48), np.int32)
    for yl, x, core, yh, z in np.ndindex(*SIZES):
        row = out[device(yl, x, core, yh, z)]
        for slot, (dy, dx, dc) in enumerate(SLOTS):
            row[slot] = (core ^ dc) * 8 + (x + dx) % 4 * 2 + (yl ^ dy)
            row[24 + slot] = ((yl ^ dy) * 4 + (x + dx) % 4) * 2 + (core ^ dc)
        for k in range(8):
            row[16 + k] = (yl ^ (k % 2)) * 4 + (x + k // 2) % 4
        row[40] = (x - z // 2) % 4 * 2 + (yl ^ (z % 2))
    return out


def visible(ids):
    frame = jnp.repeat(ids, GROUP)
    patch = jnp.tile(jnp.arange(GROUP, dtype=jnp.int32), FRAMES)
    allowed = (frame[None, :] <= frame[:, None]) & (patch[None, :] == patch[:, None])
    return allowed.astype(jnp.float32)


VMEM = pl.BlockSpec(memory_space=pltpu.VMEM)
SMEM = pl.BlockSpec(memory_space=pltpu.SMEM)
HBM = pl.BlockSpec(memory_space=pltpu.HBM)


def load_weights(w_ref, w, sem):
    copies = []
    for chunk in range(8):
        for j in range(3):
            copies.append(
                pltpu.make_async_copy(
                    w_ref.at[chunk, j],
                    w.at[pl.ds(chunk * CHUNK, CHUNK), pl.ds(j * HEAD_DIM, HEAD_DIM)],
                    sem.at[chunk * 3 + j],
                )
            )
    for copy in copies:
        copy.start()
    return copies


def project_rows(rows, w):
    return jnp.dot(rows, w[...], preferred_element_type=jnp.float32).astype(jnp.bfloat16)


def project_kernel(count, w_ref, *refs):
    buffers, out = refs[:count], refs[count]
    tokens, result, w, w_sem, sems, o_sem = refs[count + 1 :]
    copies, at = [], 0
    loads = load_weights(w_ref, w, w_sem)
    for index, ref in enumerate(buffers):
        rows = ref.shape[0]
        copies.append(pltpu.make_async_copy(ref, tokens.at[pl.ds(at, rows)], sems.at[index]))
        copies[-1].start()
        at += rows
    for copy in loads:
        copy.wait()
    stores = []
    for index in range(0, count, 2):
        copies[index].wait()
        copies[index + 1].wait()
        groups = pl.ds(index * (PATCHES // GROUP), 2 * (PATCHES // GROUP))
        rows = project_rows(tokens[groups].reshape(2 * PATCHES, WIDTH), w)
        result[groups] = rows.reshape(-1, GROUP, COLS)
        stores.append(
            pltpu.make_async_copy(result.at[groups], out.at[groups], o_sem.at[index // 2])
        )
        stores[-1].start()
    for store in stores:
        store.wait()


def project(w, buffers):
    groups = sum(buffer.shape[0] for buffer in buffers)
    rows = groups * GROUP
    return pl.pallas_call(
        functools.partial(project_kernel, len(buffers)),
        out_shape=jax.ShapeDtypeStruct((groups, GROUP, COLS), jnp.bfloat16),
        in_specs=[HBM] * (1 + len(buffers)),
        out_specs=HBM,
        scratch_shapes=[
            pltpu.VMEM((groups, GROUP, WIDTH), jnp.bfloat16),
            pltpu.VMEM((groups, GROUP, COLS), jnp.bfloat16),
            pltpu.VMEM((WIDTH, COLS), jnp.bfloat16),
            pltpu.SemaphoreType.DMA((24,)),
            pltpu.SemaphoreType.DMA((len(buffers),)),
            pltpu.SemaphoreType.DMA((len(buffers) // 2,)),
        ],
        compiler_params=pltpu.CompilerParams(vmem_limit_bytes=58 * 2**20),
        cost_estimate=pl.CostEstimate(
            flops=2 * rows * WIDTH * COLS, bytes_accessed=2 * (rows + COLS) * WIDTH, transcendentals=0
        ),
    )(w, *buffers)


def attend(proj, grads, mask, turned):
    factor = 1.0 / math.sqrt(HEAD_DIM)
    size = FRAMES * GROUP

    def body(step, carry):
        part = proj[step].reshape(size, COLS)
        query, key, value = (part[:, j * HEAD_DIM : (j + 1) * HEAD_DIM] for j in range(3))
        grad = grads[step].reshape(size, HEAD_DIM)
        across = (((1,), (1,)), ((), ()))
        down = (((0,), (0,)), ((), ()))
        dot = functools.partial(lax.dot_general, preferred_element_type=jnp.float32)
        scores = dot(query, key, across) * factor
        scores = jnp.where(mask[...] > 0.5, scores, -1e30)
        exponent = jnp.exp(scores - jnp.max(scores, axis=-1, keepdims=True))
        probs = exponent / jnp.sum(exponent, axis=-1, keepdims=True)
        grad_probs = dot(grad, value, across)
        row_dot = jnp.sum(grad_probs * probs, axis=-1, keepdims=True)
        grad_scores = (probs * (grad_probs - row_dot)).astype(jnp.bfloat16)
        probs_b = probs.astype(jnp.bfloat16)
        grad_query = jnp.dot(grad_scores, key, preferred_element_type=jnp.float32) * factor
        grad_key = dot(grad_scores, query, down) * factor
        grad_value = dot(probs_b, grad, down)
        columns = pl.ds(pl.multiple_of(step * size, size), size)
        for j, result in enumerate((grad_query, grad_key, grad_value)):
            turned[j * HEAD_DIM : (j + 1) * HEAD_DIM, columns] = result.T.astype(jnp.bfloat16)
        return carry

    lax.fori_loop(0, PATCHES // GROUP, body, 0)


def share_kernel(count, order, mask, w_ref, g_ref, early, *refs):
    buffers, out = refs[:count], refs[count]
    tokens, proj, grads, turned, w, shares, w_sem, x_sem, g_sem, p_sem, o_sem = refs[count + 1 :]
    token_copies = []
    for index, (buffer, at, slot, first, groups) in enumerate(parts_of(FIRST + SECOND + THIRD)):
        token_copies.append(
            pltpu.make_async_copy(
                buffers[buffer].at[pl.ds(at, groups)],
                tokens.at[pl.ds(first, groups), slot],
                x_sem.at[index],
            )
        )
    last = token_copies[-len(THIRD) :]
    for copy in last:
        copy.start()
    loads = load_weights(w_ref, w, w_sem)
    small = []
    for slot in range(FRAMES):
        small.append(pltpu.make_async_copy(g_ref.at[order[slot]], grads.at[:, slot], g_sem.at[slot]))
    at = 0
    for index, (_, _, slot, first, groups) in enumerate(parts_of(FIRST + SECOND)):
        small.append(
            pltpu.make_async_copy(
                early.at[pl.ds(at, groups)], proj.at[pl.ds(first, groups), slot], p_sem.at[index]
            )
        )
        at += groups
    for copy in small + token_copies[: -len(THIRD)]:
        copy.start()
    for copy in last + loads:
        copy.wait()
    for slot in (14, 15):
        rows = project_rows(tokens[:, slot].reshape(PATCHES, WIDTH), w)
        proj[:, slot] = rows.reshape(PATCHES // GROUP, GROUP, COLS)
    for copy in small:
        copy.wait()
    attend(proj, grads, mask, turned)
    for copy in token_copies[: -len(THIRD)]:
        copy.wait()

    def weigh(step, carry):
        columns = pl.ds(pl.multiple_of(order[16 + step] * CHUNK, CHUNK), CHUNK)
        rows = tokens[:, :, :, columns].reshape(ROWS, CHUNK)
        value = jnp.dot(turned[...], rows, preferred_element_type=jnp.float32)
        for j in range(3):
            shares[step, j] = value[j * HEAD_DIM : (j + 1) * HEAD_DIM].T.astype(jnp.bfloat16)
        pltpu.make_async_copy(shares.at[step], out.at[step], o_sem.at[step]).start()
        return carry

    lax.fori_loop(0, 8, weigh, 0)
    for step in range(8):
        pltpu.make_async_copy(shares.at[step], out.at[step], o_sem.at[step]).wait()


def weight_share(order, mask, w, g, early, buffers):
    count = len(buffers)
    groups = PATCHES // GROUP
    token_parts = len(parts_of(FIRST + SECOND + THIRD))
    return pl.pallas_call(
        functools.partial(share_kernel, count),
        out_shape=jax.ShapeDtypeStruct((8, 3, CHUNK, HEAD_DIM), jnp.bfloat16),
        in_specs=[SMEM, VMEM] + [HBM] * (3 + count),
        out_specs=HBM,
        scratch_shapes=[
            pltpu.VMEM((groups, FRAMES, GROUP, WIDTH), jnp.bfloat16),
            pltpu.VMEM((groups, FRAMES, GROUP, COLS), jnp.bfloat16),
            pltpu.VMEM((groups, FRAMES, GROUP, HEAD_DIM), jnp.bfloat16),
            pltpu.VMEM((COLS, ROWS), jnp.bfloat16),
            pltpu.VMEM((WIDTH, COLS), jnp.bfloat16),
            pltpu.VMEM((8, 3, CHUNK, HEAD_DIM), jnp.bfloat16),
            pltpu.SemaphoreType.DMA((24,)),
            pltpu.SemaphoreType.DMA((token_parts,)),
            pltpu.SemaphoreType.DMA((FRAMES,)),
            pltpu.SemaphoreType.DMA((len(FIRST + SECOND),)),
            pltpu.SemaphoreType.DMA((8,)),
        ],
        compiler_params=pltpu.CompilerParams(vmem_limit_bytes=58 * 2**20),
        cost_estimate=pl.CostEstimate(
            flops=2 * ROWS * WIDTH * COLS, bytes_accessed=2 * ROWS * WIDTH, transcendentals=0
        ),
    )(order, mask, w, g, early, *buffers)


def local(inputs, grad_attn, w_qkv):
    table = jnp.asarray(tables())[lax.axis_index(AXES)]
    to_worker = [(target, source) for source, target in owner_moves(0)]
    rows_w = lax.dynamic_slice(
        w_qkv.transpose(1, 0, 2), (0, table[40] * CHUNK, 0), (3, CHUNK, HEAD_DIM)
    )
    rows_w = lax.ppermute(rows_w.reshape(3 * CHUNK, HEAD_DIM), AXES, to_worker)
    w = lax.all_gather(rows_w, "z", axis=0, tiled=True).reshape(8, 3, CHUNK, HEAD_DIM)
    exchange = lambda value, axes: lax.all_to_all(
        value, axes, split_axis=0, concat_axis=0, tiled=True
    )
    heads_g = exchange(grad_attn[0].reshape(FRAMES, PATCHES, HEAD_DIM), TOK)
    frames_g = exchange(heads_g, ("core", "x", "yl"))
    steps = gather_frames(inputs[0], (rows_w, heads_g), (frames_g,))
    g = frames_g.reshape(FRAMES, PATCHES // GROUP, GROUP, HEAD_DIM)
    first, second, third = (
        [buffer.reshape(-1, GROUP, WIDTH) for buffer in buffers] for buffers in steps
    )
    early = project(w, first + second)
    share = weight_share(table[:24], visible(table[24:40]), w, g, early, first + second + third)
    mine = lax.psum_scatter(
        share.reshape(8 * 3 * CHUNK, HEAD_DIM), "z", scatter_dimension=0, tiled=True
    )
    mine = mine.reshape(3, 2, CHUNK // 2, HEAD_DIM)
    yh = lax.axis_index("yh")
    total = None
    for flip in range(2):
        part = lax.dynamic_index_in_dim(mine, (yh + flip) % 2, 1, keepdims=False)
        part = lax.ppermute(part, AXES, owner_moves(flip)).astype(jnp.float32)
        total = part if total is None else total + part
    return total.astype(jnp.bfloat16).transpose(1, 0, 2)


def solution(mesh):
    fine = Mesh(mesh.devices.reshape(SIZES), AXES)
    in_specs = (P(FRAME, TOK, None), P(FRAME, None, TOK), P(None, None, TOK))
    out_specs = P(FRAME, None, TOK)
    return jax.shard_map(local, mesh=fine, in_specs=in_specs, out_specs=out_specs, check_vma=False)
```

```python
import functools
import math

import jax
import jax.numpy as jnp
import numpy as np
from jax import lax
from jax.experimental import pallas as pl
from jax.experimental.pallas import tpu as pltpu
from jax.sharding import Mesh, PartitionSpec as P

HEAD_DIM = 128
AXES = ("yl", "x", "core", "yh", "z")
SIZES = (2, 4, 2, 2, 8)
FRAME = AXES[:3]
TOK = AXES[3:]
FRAMES = 16
PATCHES = 128
CUT_A, CUT_B = 48, 96
CUTS = ((0, CUT_A), (CUT_A, CUT_B), (CUT_B, PATCHES))
STEP = 4
CUT_FLOPS = 3 * 10**10
WIDTH = 4096
COLS = 3 * HEAD_DIM
ROWS = FRAMES * PATCHES
GROUP = 16
CHUNK = WIDTH // 8

SAME_CORE = ((0, 0), (0, 1), (0, -1), (1, 0), (0, 2), (1, 1), (1, -1), (1, 2))
SLOTS = [(dy, dx, dc) for dy, dx in SAME_CORE for dc in (0, 1)]


def device(yl, x, core, yh, z):
    place = 0
    for value, size in zip((yl, x, core, yh, z), SIZES):
        place = place * size + value % size
    return place


def worker_moves():
    pairs = []
    for yl, x, core, yh, z in np.ndindex(*SIZES):
        owner = device(yl ^ (z % 2), x + z // 2, yh, core, 2 * x + yl)
        pairs.append((owner, device(yl, x, core, yh, z)))
    return pairs


def plane_moves(flip):
    pairs = []
    for yl, x, core, yh, z in np.ndindex(*SIZES):
        target = device(yl ^ (z % 2), x + z // 2, yh ^ flip, core, z)
        pairs.append((device(yl, x, core, yh, z), target))
    return pairs


def line_moves():
    pairs = []
    for yl, x, core, yh, z in np.ndindex(*SIZES):
        target = device(yl, x, core, yh, 2 * ((x - z // 2) % 4) + (yl ^ (z % 2)))
        pairs.append((device(yl, x, core, yh, z), target))
    return pairs


def shift(value, axis, by):
    count = SIZES[AXES.index(axis)]
    return lax.ppermute(value, axis, [(i, (i + by) % count) for i in range(count)])


def after(values, *others):
    return lax.optimization_barrier((values, *others))[0]


def cut_kernel(*refs):
    sems = refs[-1]
    copies = []
    for index, (first, last) in enumerate(CUTS):
        source, target = refs[index], refs[3 + index]
        copies.append(
            pltpu.make_async_copy(source.at[pl.ds(first, last - first)], target, sems.at[index])
        )
        copies[-1].start()
    for copy in copies:
        copy.wait()


def cut(*buffers):
    hbm = pl.BlockSpec(memory_space=pltpu.HBM)
    return pl.pallas_call(
        cut_kernel,
        out_shape=[
            jax.ShapeDtypeStruct((last - first, WIDTH), jnp.bfloat16) for first, last in CUTS
        ],
        in_specs=[hbm] * 3,
        out_specs=[pl.BlockSpec(memory_space=pltpu.VMEM)] * 3,
        scratch_shapes=[pltpu.SemaphoreType.DMA((3,))],
        cost_estimate=pl.CostEstimate(flops=CUT_FLOPS, bytes_accessed=0, transcendentals=0),
    )(*buffers)


def gather_frames(own, early, middle):
    twin = lambda values: [shift(value, "core", 1) for value in values]
    first = [shift(own, "x", 1), shift(own, "x", -1), shift(own, "yl", 1)]
    own_twin = shift(own, "core", 1)
    left, right, other = after(first, *early)
    second = [shift(other, "x", 1), shift(right, "x", -1), shift(right, "yl", 1)]
    first_twins = twin([left, right, other])
    other_left, far, other_right = after(second, *middle)
    cuts = cut(other_left, other_right, far)
    third = [shift(cuts[0], "x", 1), shift(cuts[1], "x", -1), shift(cuts[2], "yl", 1)]
    second_twins = twin([other_left, far, other_right])
    third = after(third)
    return (
        [own, own_twin, left, right, other, *first_twins],
        [other_left, far, other_right, *second_twins],
        [*third, *twin(third)],
    )


FIRST = [[(slot, 0, PATCHES)] for slot in (0, 1, 4, 2, 6, 5, 3, 7)]
SECOND = [[(slot, 0, PATCHES)] for slot in (12, 8, 10, 13, 9, 11)]
THIRD = [
    [(14 + core, first, last - first)]
    for core in (0, 1)
    for first, last in CUTS
]


def parts_of(places):
    out = []
    for buffer, parts in enumerate(places):
        row = 0
        for slot, first, rows in parts:
            out.append((buffer, row // GROUP, slot, first // GROUP, rows // GROUP))
            row += rows
    return out


def tables():
    out = np.zeros((256, 48), np.int32)
    for yl, x, core, yh, z in np.ndindex(*SIZES):
        row = out[device(yl, x, core, yh, z)]
        for slot, (dy, dx, dc) in enumerate(SLOTS):
            row[slot] = (core ^ dc) * 8 + (x + dx) % 4 * 2 + (yl ^ dy)
            row[24 + slot] = ((yl ^ dy) * 4 + (x + dx) % 4) * 2 + (core ^ dc)
        for k in range(8):
            row[16 + k] = (yl ^ (k % 2)) * 4 + (x + k // 2) % 4
        row[40] = (x - z // 2) % 4 * 2 + (yl ^ (z % 2))
    return out


def visible(ids):
    frame = jnp.repeat(ids, GROUP)
    patch = jnp.tile(jnp.arange(GROUP, dtype=jnp.int32), FRAMES)
    allowed = (frame[None, :] <= frame[:, None]) & (patch[None, :] == patch[:, None])
    return allowed.astype(jnp.float32)


VMEM = pl.BlockSpec(memory_space=pltpu.VMEM)
SMEM = pl.BlockSpec(memory_space=pltpu.SMEM)
HBM = pl.BlockSpec(memory_space=pltpu.HBM)


def take_kernel(start, w_ref, out, sem):
    copies = []
    for j in range(3):
        rows = pl.ds(pl.multiple_of(start[0] * CHUNK, CHUNK), CHUNK)
        columns = pl.ds(j * HEAD_DIM, HEAD_DIM)
        copies.append(pltpu.make_async_copy(w_ref.at[j, rows], out.at[:, columns], sem.at[j]))
        copies[-1].start()
    for copy in copies:
        copy.wait()


def take_rows(start, w):
    return pl.pallas_call(
        take_kernel,
        out_shape=jax.ShapeDtypeStruct((CHUNK, COLS), jnp.bfloat16),
        in_specs=[SMEM, HBM],
        out_specs=VMEM,
        scratch_shapes=[pltpu.SemaphoreType.DMA((3,))],
    )(start, w)


def attend(proj, grads, mask, turned):
    factor = 1.0 / math.sqrt(HEAD_DIM)
    size = FRAMES * GROUP

    def body(step, carry):
        part = proj[step].reshape(size, COLS)
        query, key, value = (part[:, j * HEAD_DIM : (j + 1) * HEAD_DIM] for j in range(3))
        grad = grads[step].reshape(size, HEAD_DIM)
        across = (((1,), (1,)), ((), ()))
        down = (((0,), (0,)), ((), ()))
        dot = functools.partial(lax.dot_general, preferred_element_type=jnp.float32)
        scores = dot(query, key, across) * factor
        scores = jnp.where(mask[...] > 0.5, scores, -1e30)
        exponent = jnp.exp(scores - jnp.max(scores, axis=-1, keepdims=True))
        probs = exponent / jnp.sum(exponent, axis=-1, keepdims=True)
        grad_probs = dot(grad, value, across)
        row_dot = jnp.sum(grad_probs * probs, axis=-1, keepdims=True)
        grad_scores = (probs * (grad_probs - row_dot)).astype(jnp.bfloat16)
        probs_b = probs.astype(jnp.bfloat16)
        grad_query = jnp.dot(grad_scores, key, preferred_element_type=jnp.float32) * factor
        grad_key = dot(grad_scores, query, down) * factor
        grad_value = dot(probs_b, grad, down)
        columns = pl.ds(pl.multiple_of(step * size, size), size)
        for j, result in enumerate((grad_query, grad_key, grad_value)):
            turned[j * HEAD_DIM : (j + 1) * HEAD_DIM, columns] = result.T.astype(jnp.bfloat16)
        return carry

    lax.fori_loop(0, PATCHES // GROUP, body, 0)


def share_kernel(count, order, mask, w_ref, g_ref, *refs):
    buffers, out = refs[:count], refs[count]
    tokens, proj, grads, turned, w, shares, w_sem, x_sem, g_sem, o_sem = refs[count + 1 :]
    arrivals = [[] for _ in range(FRAMES)]
    for index, (buffer, at, slot, first, groups) in enumerate(parts_of(FIRST + SECOND + THIRD)):
        arrivals[slot].append(
            pltpu.make_async_copy(
                buffers[buffer].at[pl.ds(at, groups)],
                tokens.at[pl.ds(first, groups), slot],
                x_sem.at[index],
            )
        )
    cotangents = []
    for slot in range(FRAMES):
        cotangents.append(
            pltpu.make_async_copy(g_ref.at[order[slot]], grads.at[:, slot], g_sem.at[slot])
        )
    weights = pltpu.make_async_copy(w_ref, w, w_sem.at[0])

    def step_copies(step):
        return [copy for slot in range(STEP * step, STEP * step + STEP) for copy in arrivals[slot]]

    weights.start()
    for copy in step_copies(0):
        copy.start()
    weights.wait()
    steps = FRAMES // STEP
    for step in range(steps):
        for copy in step_copies(step):
            copy.wait()
        for copy in step_copies(step + 1) if step + 1 < steps else cotangents:
            copy.start()
        slots = slice(STEP * step, STEP * step + STEP)
        rows = tokens[:, slots].reshape(STEP * PATCHES, WIDTH)
        result = jnp.dot(rows, w[...], preferred_element_type=jnp.float32)
        proj[:, slots] = result.astype(jnp.bfloat16).reshape(-1, STEP, GROUP, COLS)
    for copy in cotangents:
        copy.wait()
    attend(proj, grads, mask, turned)

    def weigh(step, carry):
        columns = pl.ds(pl.multiple_of(order[16 + step] * CHUNK, CHUNK), CHUNK)
        rows = tokens[:, :, :, columns].reshape(ROWS, CHUNK)
        value = jnp.dot(turned[...], rows, preferred_element_type=jnp.float32)
        for j in range(3):
            shares[step, j] = value[j * HEAD_DIM : (j + 1) * HEAD_DIM].T.astype(jnp.bfloat16)
        pltpu.make_async_copy(shares.at[step], out.at[step], o_sem.at[step]).start()
        return carry

    lax.fori_loop(0, 8, weigh, 0)
    for step in range(8):
        pltpu.make_async_copy(shares.at[step], out.at[step], o_sem.at[step]).wait()


def weight_share(order, mask, w, g, buffers):
    count = len(buffers)
    groups = PATCHES // GROUP
    return pl.pallas_call(
        functools.partial(share_kernel, count),
        out_shape=jax.ShapeDtypeStruct((8, 3, CHUNK, HEAD_DIM), jnp.bfloat16),
        in_specs=[SMEM, VMEM] + [HBM] * (2 + count),
        out_specs=HBM,
        scratch_shapes=[
            pltpu.VMEM((groups, FRAMES, GROUP, WIDTH), jnp.bfloat16),
            pltpu.VMEM((groups, FRAMES, GROUP, COLS), jnp.bfloat16),
            pltpu.VMEM((groups, FRAMES, GROUP, HEAD_DIM), jnp.bfloat16),
            pltpu.VMEM((COLS, ROWS), jnp.bfloat16),
            pltpu.VMEM((WIDTH, COLS), jnp.bfloat16),
            pltpu.VMEM((8, 3, CHUNK, HEAD_DIM), jnp.bfloat16),
            pltpu.SemaphoreType.DMA((1,)),
            pltpu.SemaphoreType.DMA((len(parts_of(FIRST + SECOND + THIRD)),)),
            pltpu.SemaphoreType.DMA((FRAMES,)),
            pltpu.SemaphoreType.DMA((8,)),
        ],
        compiler_params=pltpu.CompilerParams(vmem_limit_bytes=58 * 2**20),
        cost_estimate=pl.CostEstimate(
            flops=4 * ROWS * WIDTH * COLS, bytes_accessed=2 * ROWS * WIDTH, transcendentals=0
        ),
    )(order, mask, w, g, *buffers)


def local(inputs, grad_attn, w_qkv):
    table = jnp.asarray(tables())[lax.axis_index(AXES)]
    rows_w = take_rows(table[40:41], w_qkv.transpose(1, 0, 2))
    rows_w = lax.ppermute(rows_w, AXES, worker_moves())
    w = lax.all_gather(rows_w, "z", axis=0, tiled=True)
    exchange = lambda value, axes: lax.all_to_all(
        value, axes, split_axis=0, concat_axis=0, tiled=True
    )
    heads_g = exchange(after(grad_attn[0], rows_w).reshape(FRAMES, PATCHES, HEAD_DIM), TOK)
    frames_g = exchange(heads_g, ("core", "x", "yl"))
    steps = gather_frames(inputs[0], (rows_w,), (heads_g,))
    g = frames_g.reshape(FRAMES, PATCHES // GROUP, GROUP, HEAD_DIM)
    first, second, third = (
        [buffer.reshape(-1, GROUP, WIDTH) for buffer in buffers] for buffers in steps
    )
    share = weight_share(table[:24], visible(table[24:40]), w, g, first + second + third)
    mine = lax.psum_scatter(
        share.reshape(8 * 3 * CHUNK, HEAD_DIM), "z", scatter_dimension=0, tiled=True
    )
    mine = mine.reshape(3, 2, CHUNK // 2, HEAD_DIM)
    yh = lax.axis_index("yh")
    total = None
    for flip in range(2):
        part = lax.dynamic_index_in_dim(mine, (yh + flip) % 2, 1, keepdims=False)
        part = lax.ppermute(part, AXES, plane_moves(flip)).astype(jnp.float32)
        total = part if total is None else total + part
    return lax.ppermute(total.astype(jnp.bfloat16), AXES, line_moves()).transpose(1, 0, 2)


def solution(mesh):
    fine = Mesh(mesh.devices.reshape(SIZES), AXES)
    in_specs = (P(FRAME, TOK, None), P(FRAME, None, TOK), P(None, None, TOK))
    out_specs = P(FRAME, None, TOK)
    return jax.shard_map(local, mesh=fine, in_specs=in_specs, out_specs=out_specs, check_vma=False)
```

```python
import functools
import math

import jax
import jax.numpy as jnp
import numpy as np
from jax import lax
from jax.experimental import pallas as pl
from jax.experimental.pallas import tpu as pltpu
from jax.sharding import Mesh, PartitionSpec as P

HEAD_DIM = 128
AXES = ("yl", "x", "core", "yh", "z")
SIZES = (2, 4, 2, 2, 8)
FRAME = AXES[:3]
TOK = AXES[3:]
FRAMES = 16
PATCHES = 128
CUT_A, CUT_B = 48, 96
CUTS = ((0, CUT_A), (CUT_A, CUT_B), (CUT_B, PATCHES))
STEP = 4
FAR = (4, 5)
NEAR = (3, 6, 2, 7, 1, 0)
CUT_FLOPS = 3 * 10**10
WIDTH = 4096
COLS = 3 * HEAD_DIM
ROWS = FRAMES * PATCHES
GROUP = 16
CHUNK = WIDTH // 8

SAME_CORE = ((0, 0), (0, 1), (0, -1), (1, 0), (0, 2), (1, 1), (1, -1), (1, 2))
SLOTS = [(dy, dx, dc) for dy, dx in SAME_CORE for dc in (0, 1)]


def device(yl, x, core, yh, z):
    place = 0
    for value, size in zip((yl, x, core, yh, z), SIZES):
        place = place * size + value % size
    return place


def worker_moves():
    pairs = []
    for yl, x, core, yh, z in np.ndindex(*SIZES):
        owner = device(yl ^ (z % 2), x + z // 2, yh, core, 2 * x + yl)
        pairs.append((owner, device(yl, x, core, yh, z)))
    return pairs


def plane_moves(flip):
    pairs = []
    for yl, x, core, yh, z in np.ndindex(*SIZES):
        target = device(yl ^ (z % 2), x + z // 2, yh ^ flip, core, z)
        pairs.append((device(yl, x, core, yh, z), target))
    return pairs


def line_moves():
    pairs = []
    for yl, x, core, yh, z in np.ndindex(*SIZES):
        target = device(yl, x, core, yh, 2 * ((x - z // 2) % 4) + (yl ^ (z % 2)))
        pairs.append((device(yl, x, core, yh, z), target))
    return pairs


def shift(value, axis, by):
    count = SIZES[AXES.index(axis)]
    return lax.ppermute(value, axis, [(i, (i + by) % count) for i in range(count)])


def after(values, *others):
    return lax.optimization_barrier((values, *others))[0]


def cut_kernel(*refs):
    sems = refs[-1]
    copies = []
    for index, (first, last) in enumerate(CUTS):
        source, target = refs[index], refs[3 + index]
        copies.append(
            pltpu.make_async_copy(source.at[pl.ds(first, last - first)], target, sems.at[index])
        )
        copies[-1].start()
    for copy in copies:
        copy.wait()


def cut(*buffers):
    hbm = pl.BlockSpec(memory_space=pltpu.HBM)
    return pl.pallas_call(
        cut_kernel,
        out_shape=[
            jax.ShapeDtypeStruct((last - first, WIDTH), jnp.bfloat16) for first, last in CUTS
        ],
        in_specs=[hbm] * 3,
        out_specs=[pl.BlockSpec(memory_space=pltpu.VMEM)] * 3,
        scratch_shapes=[pltpu.SemaphoreType.DMA((3,))],
        cost_estimate=pl.CostEstimate(flops=CUT_FLOPS, bytes_accessed=0, transcendentals=0),
    )(*buffers)


def gather_frames(own, early, middle, late):
    twin = lambda values: [shift(value, "core", 1) for value in values]
    first = [shift(own, "x", 1), shift(own, "x", -1), shift(own, "yl", 1)]
    own_twin = shift(own, "core", 1)
    left, right, other = after(first, *early)
    second = [shift(other, "x", 1), shift(right, "x", -1), shift(right, "yl", 1)]
    first_twins = twin([left, right, other])
    other_left, far, other_right = after(second, *middle)
    cuts = cut(other_left, other_right, far)
    third = [shift(cuts[0], "x", 1), shift(cuts[1], "x", -1), shift(cuts[2], "yl", 1)]
    second_twins = twin([other_left, far, other_right])
    third = after(third, *late)
    return (
        [own, own_twin, left, right, other, *first_twins],
        [other_left, far, other_right, *second_twins],
        [*third, *twin(third)],
    )


FIRST = [[(slot, 0, PATCHES)] for slot in (0, 1, 4, 2, 6, 5, 3, 7)]
SECOND = [[(slot, 0, PATCHES)] for slot in (12, 8, 10, 13, 9, 11)]
THIRD = [
    [(14 + core, first, last - first)]
    for core in (0, 1)
    for first, last in CUTS
]


def parts_of(places):
    out = []
    for buffer, parts in enumerate(places):
        row = 0
        for slot, first, rows in parts:
            out.append((buffer, row // GROUP, slot, first // GROUP, rows // GROUP))
            row += rows
    return out


PARTS = parts_of(FIRST + SECOND + THIRD)


def tables():
    out = np.zeros((256, 48), np.int32)
    for yl, x, core, yh, z in np.ndindex(*SIZES):
        row = out[device(yl, x, core, yh, z)]
        for slot, (dy, dx, dc) in enumerate(SLOTS):
            row[slot] = (core ^ dc) * 8 + (x + dx) % 4 * 2 + (yl ^ dy)
            row[24 + slot] = ((yl ^ dy) * 4 + (x + dx) % 4) * 2 + (core ^ dc)
        for k in range(8):
            at = (z + k) % 8
            row[16 + k] = (yl ^ (at % 2)) * 4 + (x + at // 2) % 4
        row[40] = (x - z // 2) % 4 * 2 + (yl ^ (z % 2))
    return out


def visible(ids):
    frame = jnp.repeat(ids, GROUP)
    patch = jnp.tile(jnp.arange(GROUP, dtype=jnp.int32), FRAMES)
    allowed = (frame[None, :] <= frame[:, None]) & (patch[None, :] == patch[:, None])
    return allowed.astype(jnp.float32)


VMEM = pl.BlockSpec(memory_space=pltpu.VMEM)
SMEM = pl.BlockSpec(memory_space=pltpu.SMEM)
HBM = pl.BlockSpec(memory_space=pltpu.HBM)


def take_kernel(start, w_ref, out, sem):
    copies = []
    for j in range(3):
        rows = pl.ds(pl.multiple_of(start[0] * CHUNK, CHUNK), CHUNK)
        columns = pl.ds(j * HEAD_DIM, HEAD_DIM)
        copies.append(pltpu.make_async_copy(w_ref.at[j, rows], out.at[:, columns], sem.at[j]))
        copies[-1].start()
    for copy in copies:
        copy.wait()


def take_rows(start, w):
    return pl.pallas_call(
        take_kernel,
        out_shape=jax.ShapeDtypeStruct((CHUNK, COLS), jnp.bfloat16),
        in_specs=[SMEM, HBM],
        out_specs=VMEM,
        scratch_shapes=[pltpu.SemaphoreType.DMA((3,))],
    )(start, w)


def attend(proj, grads, mask, turned):
    factor = 1.0 / math.sqrt(HEAD_DIM)
    size = FRAMES * GROUP

    def body(step, carry):
        part = proj[step].reshape(size, COLS)
        query, key, value = (part[:, j * HEAD_DIM : (j + 1) * HEAD_DIM] for j in range(3))
        grad = grads[step].reshape(size, HEAD_DIM)
        across = (((1,), (1,)), ((), ()))
        down = (((0,), (0,)), ((), ()))
        dot = functools.partial(lax.dot_general, preferred_element_type=jnp.float32)
        scores = dot(query, key, across) * factor
        scores = jnp.where(mask[...] > 0.5, scores, -1e30)
        exponent = jnp.exp(scores - jnp.max(scores, axis=-1, keepdims=True))
        probs = exponent / jnp.sum(exponent, axis=-1, keepdims=True)
        grad_probs = dot(grad, value, across)
        row_dot = jnp.sum(grad_probs * probs, axis=-1, keepdims=True)
        grad_scores = (probs * (grad_probs - row_dot)).astype(jnp.bfloat16)
        probs_b = probs.astype(jnp.bfloat16)
        grad_query = jnp.dot(grad_scores, key, preferred_element_type=jnp.float32) * factor
        grad_key = dot(grad_scores, query, down) * factor
        grad_value = dot(probs_b, grad, down)
        columns = pl.ds(pl.multiple_of(step * size, size), size)
        for j, result in enumerate((grad_query, grad_key, grad_value)):
            turned[j * HEAD_DIM : (j + 1) * HEAD_DIM, columns] = result.T.astype(jnp.bfloat16)
        return carry

    lax.fori_loop(0, PATCHES // GROUP, body, 0)


def share_kernel(count, order, mask, w_ref, g_ref, *refs):
    buffers, turned_out, out = refs[:count], refs[count], refs[count + 1 : count + 1 + len(FAR)]
    tokens, proj, grads, turned, w, w_sem, x_sem, g_sem = refs[count + 1 + len(FAR) :]
    arrivals = [[] for _ in range(FRAMES)]
    for index, (buffer, at, slot, first, groups) in enumerate(PARTS):
        arrivals[slot].append(
            pltpu.make_async_copy(
                buffers[buffer].at[pl.ds(at, groups)],
                tokens.at[pl.ds(first, groups), slot],
                x_sem.at[index],
            )
        )
    cotangents = []
    for slot in range(FRAMES):
        cotangents.append(
            pltpu.make_async_copy(g_ref.at[order[slot]], grads.at[:, slot], g_sem.at[slot])
        )
    weights = pltpu.make_async_copy(w_ref, w, w_sem.at[0])

    def step_copies(step):
        return [copy for slot in range(STEP * step, STEP * step + STEP) for copy in arrivals[slot]]

    weights.start()
    for copy in step_copies(0):
        copy.start()
    weights.wait()
    steps = FRAMES // STEP
    for step in range(steps):
        for copy in step_copies(step):
            copy.wait()
        for copy in step_copies(step + 1) if step + 1 < steps else cotangents:
            copy.start()
        slots = slice(STEP * step, STEP * step + STEP)
        rows = tokens[:, slots].reshape(STEP * PATCHES, WIDTH)
        result = jnp.dot(rows, w[...], preferred_element_type=jnp.float32)
        proj[:, slots] = result.astype(jnp.bfloat16).reshape(-1, STEP, GROUP, COLS)
    for copy in cotangents:
        copy.wait()
    attend(proj, grads, mask, turned)
    store = pltpu.make_async_copy(turned, turned_out, w_sem.at[1])
    store.start()
    for index, ahead in enumerate(FAR):
        columns = pl.ds(pl.multiple_of(order[16 + ahead] * CHUNK, CHUNK), CHUNK)
        rows = tokens[:, :, :, columns].reshape(ROWS, CHUNK)
        weigh(turned, rows, out[index])
    store.wait()


def weigh(turned, rows, out):
    value = jnp.dot(turned[...], rows, preferred_element_type=jnp.float32)
    for j in range(3):
        out[j] = value[j * HEAD_DIM : (j + 1) * HEAD_DIM].T.astype(jnp.bfloat16)


def near_kernel(count, order, turned_ref, *refs):
    buffers, out = refs[:count], refs[count : count + len(NEAR)]
    tokens, turned, t_sem, x_sem = refs[count + len(NEAR) :]
    load = pltpu.make_async_copy(turned_ref, turned, t_sem.at[0])
    load.start()
    copies = []
    for index, ahead in enumerate(NEAR):
        columns = pl.ds(pl.multiple_of(order[16 + ahead] * CHUNK, CHUNK), CHUNK)
        copies.append([])
        for part, (buffer, at, slot, first, groups) in enumerate(PARTS):
            copies[-1].append(
                pltpu.make_async_copy(
                    buffers[buffer].at[pl.ds(at, groups), :, columns],
                    tokens.at[index, pl.ds(first, groups), slot],
                    x_sem.at[index, part],
                )
            )
    for copy in copies[0] + copies[1]:
        copy.start()
    load.wait()
    for index in range(len(NEAR)):
        for copy in copies[index]:
            copy.wait()
        if index + 2 < len(NEAR):
            for copy in copies[index + 2]:
                copy.start()
        weigh(turned, tokens[index].reshape(ROWS, CHUNK), out[index])


def near_shares(order, turned, buffers):
    count = len(buffers)
    share = jax.ShapeDtypeStruct((3, CHUNK, HEAD_DIM), jnp.bfloat16)
    return pl.pallas_call(
        functools.partial(near_kernel, count),
        out_shape=[share] * len(NEAR),
        in_specs=[SMEM] + [HBM] * (1 + count),
        out_specs=[VMEM] * len(NEAR),
        scratch_shapes=[
            pltpu.VMEM((len(NEAR), PATCHES // GROUP, FRAMES, GROUP, CHUNK), jnp.bfloat16),
            pltpu.VMEM((COLS, ROWS), jnp.bfloat16),
            pltpu.SemaphoreType.DMA((1,)),
            pltpu.SemaphoreType.DMA((len(NEAR), len(PARTS))),
        ],
        compiler_params=pltpu.CompilerParams(vmem_limit_bytes=44 * 2**20),
        cost_estimate=pl.CostEstimate(
            flops=2 * ROWS * len(NEAR) * CHUNK * COLS,
            bytes_accessed=2 * ROWS * len(NEAR) * CHUNK,
            transcendentals=0,
        ),
    )(order, turned, *buffers)


def far_shares(order, mask, w, g, buffers):
    count = len(buffers)
    groups = PATCHES // GROUP
    share = jax.ShapeDtypeStruct((3, CHUNK, HEAD_DIM), jnp.bfloat16)
    return pl.pallas_call(
        functools.partial(share_kernel, count),
        out_shape=[jax.ShapeDtypeStruct((COLS, ROWS), jnp.bfloat16)] + [share] * len(FAR),
        in_specs=[SMEM, VMEM] + [HBM] * (2 + count),
        out_specs=[HBM] + [VMEM] * len(FAR),
        scratch_shapes=[
            pltpu.VMEM((groups, FRAMES, GROUP, WIDTH), jnp.bfloat16),
            pltpu.VMEM((groups, FRAMES, GROUP, COLS), jnp.bfloat16),
            pltpu.VMEM((groups, FRAMES, GROUP, HEAD_DIM), jnp.bfloat16),
            pltpu.VMEM((COLS, ROWS), jnp.bfloat16),
            pltpu.VMEM((WIDTH, COLS), jnp.bfloat16),
            pltpu.SemaphoreType.DMA((2,)),
            pltpu.SemaphoreType.DMA((len(PARTS),)),
            pltpu.SemaphoreType.DMA((FRAMES,)),
        ],
        compiler_params=pltpu.CompilerParams(vmem_limit_bytes=44 * 2**20),
        cost_estimate=pl.CostEstimate(
            flops=2 * ROWS * WIDTH * COLS, bytes_accessed=2 * ROWS * WIDTH, transcendentals=0
        ),
    )(order, mask, w, g, *buffers)


def add(*parts):
    return sum(part.astype(jnp.float32) for part in parts).astype(jnp.bfloat16)


def local(inputs, grad_attn, w_qkv):
    table = jnp.asarray(tables())[lax.axis_index(AXES)]
    rows_w = take_rows(table[40:41], w_qkv.transpose(1, 0, 2))
    rows_w = lax.ppermute(rows_w, AXES, worker_moves())
    w = lax.all_gather(rows_w, "z", axis=0, tiled=True)
    exchange = lambda value, axes: lax.all_to_all(
        value, axes, split_axis=0, concat_axis=0, tiled=True
    )
    heads_g = exchange(after(grad_attn[0], rows_w).reshape(FRAMES, PATCHES, HEAD_DIM), TOK)
    frames_g = exchange(heads_g, ("core", "x", "yl"))
    steps = gather_frames(inputs[0], (rows_w,), (heads_g,), (frames_g,))
    g = frames_g.reshape(FRAMES, PATCHES // GROUP, GROUP, HEAD_DIM)
    first, second, third = (
        [buffer.reshape(-1, GROUP, WIDTH) for buffer in buffers] for buffers in steps
    )
    order, buffers = table[:24], first + second + third
    turned, up, down = far_shares(order, visible(table[24:40]), w, g, buffers)
    up, down, near = lax.optimization_barrier(
        (shift(up, "z", 1), shift(down, "z", -1), near_shares(order, turned, buffers))
    )
    for step in (0, 2):
        up = shift(add(up, near[step]), "z", 1)
        down = shift(add(down, near[step + 1]), "z", -1)
    up = shift(add(up, near[4]), "z", 1)
    mine = add(up, down, near[5])
    mine = mine.reshape(3, 2, CHUNK // 2, HEAD_DIM)
    yh = lax.axis_index("yh")
    total = None
    for flip in range(2):
        part = lax.dynamic_index_in_dim(mine, (yh + flip) % 2, 1, keepdims=False)
        part = lax.ppermute(part, AXES, plane_moves(flip)).astype(jnp.float32)
        total = part if total is None else total + part
    return lax.ppermute(total.astype(jnp.bfloat16), AXES, line_moves()).transpose(1, 0, 2)


def solution(mesh):
    fine = Mesh(mesh.devices.reshape(SIZES), AXES)
    in_specs = (P(FRAME, TOK, None), P(FRAME, None, TOK), P(None, None, TOK))
    out_specs = P(FRAME, None, TOK)
    return jax.shard_map(local, mesh=fine, in_specs=in_specs, out_specs=out_specs, check_vma=False)
```

```python
import functools
import math

import jax
import jax.numpy as jnp
import numpy as np
from jax import lax
from jax.experimental import pallas as pl
from jax.experimental.pallas import tpu as pltpu
from jax.sharding import Mesh, PartitionSpec as P

HEAD_DIM = 128
AXES = ("yl", "x", "core", "yh", "z")
SIZES = (2, 4, 2, 2, 8)
FRAME = AXES[:3]
TOK = AXES[3:]
FRAMES = 16
PATCHES = 128
CUT_A, CUT_B = 48, 96
CUTS = ((0, CUT_A), (CUT_A, CUT_B), (CUT_B, PATCHES))
STEP = 4
FAR = (4,)
NEAR_A = (3, 5)
NEAR_B = (2, 6, 1, 7, 0)
CUT_FLOPS = 3 * 10**10
WIDTH = 4096
COLS = 3 * HEAD_DIM
ROWS = FRAMES * PATCHES
GROUP = 16
CHUNK = WIDTH // 8
SHARE = jax.ShapeDtypeStruct((2, 3, CHUNK // 2, HEAD_DIM), jnp.bfloat16)

SAME_CORE = ((0, 0), (0, 1), (0, -1), (1, 0), (0, 2), (1, 1), (1, -1), (1, 2))
SLOTS = [(dy, dx, dc) for dy, dx in SAME_CORE for dc in (0, 1)]


def device(yl, x, core, yh, z):
    place = 0
    for value, size in zip((yl, x, core, yh, z), SIZES):
        place = place * size + value % size
    return place


def worker_moves():
    pairs = []
    for yl, x, core, yh, z in np.ndindex(*SIZES):
        owner = device(yl ^ (z % 2), x + z // 2, yh, core, 2 * x + yl)
        pairs.append((owner, device(yl, x, core, yh, z)))
    return pairs


def plane_moves(flip):
    pairs = []
    for yl, x, core, yh, z in np.ndindex(*SIZES):
        target = device(yl ^ (z % 2), x + z // 2, yh ^ flip, core, z)
        pairs.append((device(yl, x, core, yh, z), target))
    return pairs


def line_moves():
    pairs = []
    for yl, x, core, yh, z in np.ndindex(*SIZES):
        target = device(yl, x, core, yh, 2 * ((x - z // 2) % 4) + (yl ^ (z % 2)))
        pairs.append((device(yl, x, core, yh, z), target))
    return pairs


def shift(value, axis, by):
    count = SIZES[AXES.index(axis)]
    return lax.ppermute(value, axis, [(i, (i + by) % count) for i in range(count)])


def after(values, *others):
    return lax.optimization_barrier((values, *others))[0]


def cut_kernel(*refs):
    sems = refs[-1]
    copies = []
    for index, (first, last) in enumerate(CUTS):
        source, target = refs[index], refs[3 + index]
        copies.append(
            pltpu.make_async_copy(source.at[pl.ds(first, last - first)], target, sems.at[index])
        )
        copies[-1].start()
    for copy in copies:
        copy.wait()


def cut(*buffers):
    hbm = pl.BlockSpec(memory_space=pltpu.HBM)
    return pl.pallas_call(
        cut_kernel,
        out_shape=[
            jax.ShapeDtypeStruct((last - first, WIDTH), jnp.bfloat16) for first, last in CUTS
        ],
        in_specs=[hbm] * 3,
        out_specs=[pl.BlockSpec(memory_space=pltpu.VMEM)] * 3,
        scratch_shapes=[pltpu.SemaphoreType.DMA((3,))],
        cost_estimate=pl.CostEstimate(flops=CUT_FLOPS, bytes_accessed=0, transcendentals=0),
    )(*buffers)


def gather_frames(own, early, middle, late):
    twin = lambda values: [shift(value, "core", 1) for value in values]
    first = [shift(own, "x", 1), shift(own, "x", -1), shift(own, "yl", 1)]
    own_twin = shift(own, "core", 1)
    left, right, other = after(first, *early)
    second = [shift(other, "x", 1), shift(right, "x", -1), shift(right, "yl", 1)]
    first_twins = twin([left, right, other])
    other_left, far, other_right = after(second, *middle)
    cuts = cut(other_left, other_right, far)
    third = [shift(cuts[0], "x", 1), shift(cuts[1], "x", -1), shift(cuts[2], "yl", 1)]
    second_twins = twin([other_left, far, other_right])
    third = after(third, *late)
    return (
        [own, own_twin, left, right, other, *first_twins],
        [other_left, far, other_right, *second_twins],
        [*third, *twin(third)],
    )


FIRST = [[(slot, 0, PATCHES)] for slot in (0, 1, 4, 2, 6, 5, 3, 7)]
SECOND = [[(slot, 0, PATCHES)] for slot in (12, 8, 10, 13, 9, 11)]
THIRD = [
    [(14 + core, first, last - first)]
    for core in (0, 1)
    for first, last in CUTS
]


def parts_of(places):
    out = []
    for buffer, parts in enumerate(places):
        row = 0
        for slot, first, rows in parts:
            out.append((buffer, row // GROUP, slot, first // GROUP, rows // GROUP))
            row += rows
    return out


PARTS = parts_of(FIRST + SECOND + THIRD)


def tables():
    out = np.zeros((256, 48), np.int32)
    for yl, x, core, yh, z in np.ndindex(*SIZES):
        row = out[device(yl, x, core, yh, z)]
        for slot, (dy, dx, dc) in enumerate(SLOTS):
            row[slot] = (core ^ dc) * 8 + (x + dx) % 4 * 2 + (yl ^ dy)
            row[24 + slot] = ((yl ^ dy) * 4 + (x + dx) % 4) * 2 + (core ^ dc)
        for k in range(8):
            at = (z + k) % 8
            row[16 + k] = (yl ^ (at % 2)) * 4 + (x + at // 2) % 4
        row[40] = (x - z // 2) % 4 * 2 + (yl ^ (z % 2))
    return out


def visible(ids):
    frame = jnp.repeat(ids, GROUP)
    patch = jnp.tile(jnp.arange(GROUP, dtype=jnp.int32), FRAMES)
    allowed = (frame[None, :] <= frame[:, None]) & (patch[None, :] == patch[:, None])
    return allowed.astype(jnp.float32)


VMEM = pl.BlockSpec(memory_space=pltpu.VMEM)
SMEM = pl.BlockSpec(memory_space=pltpu.SMEM)
HBM = pl.BlockSpec(memory_space=pltpu.HBM)


def take_kernel(start, w_ref, out, sem):
    copies = []
    for j in range(3):
        rows = pl.ds(pl.multiple_of(start[0] * CHUNK, CHUNK), CHUNK)
        columns = pl.ds(j * HEAD_DIM, HEAD_DIM)
        copies.append(pltpu.make_async_copy(w_ref.at[j, rows], out.at[:, columns], sem.at[j]))
        copies[-1].start()
    for copy in copies:
        copy.wait()


def take_rows(start, w):
    return pl.pallas_call(
        take_kernel,
        out_shape=jax.ShapeDtypeStruct((CHUNK, COLS), jnp.bfloat16),
        in_specs=[SMEM, HBM],
        out_specs=VMEM,
        scratch_shapes=[pltpu.SemaphoreType.DMA((3,))],
    )(start, w)


def attend(proj, grads, mask, turned):
    factor = 1.0 / math.sqrt(HEAD_DIM)
    size = FRAMES * GROUP

    def body(step, carry):
        part = proj[step].reshape(size, COLS)
        query, key, value = (part[:, j * HEAD_DIM : (j + 1) * HEAD_DIM] for j in range(3))
        grad = grads[step].reshape(size, HEAD_DIM)
        across = (((1,), (1,)), ((), ()))
        down = (((0,), (0,)), ((), ()))
        dot = functools.partial(lax.dot_general, preferred_element_type=jnp.float32)
        scores = dot(query, key, across) * factor
        scores = jnp.where(mask[...] > 0.5, scores, -1e30)
        exponent = jnp.exp(scores - jnp.max(scores, axis=-1, keepdims=True))
        probs = exponent / jnp.sum(exponent, axis=-1, keepdims=True)
        grad_probs = dot(grad, value, across)
        row_dot = jnp.sum(grad_probs * probs, axis=-1, keepdims=True)
        grad_scores = (probs * (grad_probs - row_dot)).astype(jnp.bfloat16)
        probs_b = probs.astype(jnp.bfloat16)
        grad_query = jnp.dot(grad_scores, key, preferred_element_type=jnp.float32) * factor
        grad_key = dot(grad_scores, query, down) * factor
        grad_value = dot(probs_b, grad, down)
        columns = pl.ds(pl.multiple_of(step * size, size), size)
        for j, result in enumerate((grad_query, grad_key, grad_value)):
            turned[j * HEAD_DIM : (j + 1) * HEAD_DIM, columns] = result.T.astype(jnp.bfloat16)
        return carry

    lax.fori_loop(0, PATCHES // GROUP, body, 0)


def share_kernel(count, order, mask, w_ref, g_ref, *refs):
    buffers, turned_out, out = refs[:count], refs[count], refs[count + 1 : count + 1 + len(FAR)]
    tokens, proj, grads, turned, w, w_sem, x_sem, g_sem = refs[count + 1 + len(FAR) :]
    arrivals = [[] for _ in range(FRAMES)]
    for index, (buffer, at, slot, first, groups) in enumerate(PARTS):
        arrivals[slot].append(
            pltpu.make_async_copy(
                buffers[buffer].at[pl.ds(at, groups)],
                tokens.at[pl.ds(first, groups), slot],
                x_sem.at[index],
            )
        )
    cotangents = []
    for slot in range(FRAMES):
        cotangents.append(
            pltpu.make_async_copy(g_ref.at[order[slot]], grads.at[:, slot], g_sem.at[slot])
        )
    weights = pltpu.make_async_copy(w_ref, w, w_sem.at[0])

    def step_copies(step):
        return [copy for slot in range(STEP * step, STEP * step + STEP) for copy in arrivals[slot]]

    weights.start()
    for copy in step_copies(0):
        copy.start()
    weights.wait()
    steps = FRAMES // STEP
    for step in range(steps):
        for copy in step_copies(step):
            copy.wait()
        for copy in step_copies(step + 1) if step + 1 < steps else cotangents:
            copy.start()
        slots = slice(STEP * step, STEP * step + STEP)
        rows = tokens[:, slots].reshape(STEP * PATCHES, WIDTH)
        result = jnp.dot(rows, w[...], preferred_element_type=jnp.float32)
        proj[:, slots] = result.astype(jnp.bfloat16).reshape(-1, STEP, GROUP, COLS)
    for copy in cotangents:
        copy.wait()
    attend(proj, grads, mask, turned)
    store = pltpu.make_async_copy(turned, turned_out, w_sem.at[1])
    store.start()
    for index, ahead in enumerate(FAR):
        columns = pl.ds(pl.multiple_of(order[16 + ahead] * CHUNK, CHUNK), CHUNK)
        rows = tokens[:, :, :, columns].reshape(ROWS, CHUNK)
        weigh(turned, rows, out[index])
    store.wait()


def weigh(turned, rows, out):
    value = jnp.dot(turned[...], rows, preferred_element_type=jnp.float32)
    for half in range(2):
        rows = slice(half * CHUNK // 2, (half + 1) * CHUNK // 2)
        for j in range(3):
            part = value[j * HEAD_DIM : (j + 1) * HEAD_DIM, rows]
            out[half, j] = part.T.astype(jnp.bfloat16)


def near_kernel(count, near, order, turned_ref, *refs):
    buffers, out = refs[:count], refs[count : count + len(near)]
    tokens, turned, t_sem, x_sem = refs[count + len(near) :]
    load = pltpu.make_async_copy(turned_ref, turned, t_sem.at[0])
    load.start()
    copies = []
    for index, ahead in enumerate(near):
        columns = pl.ds(pl.multiple_of(order[16 + ahead] * CHUNK, CHUNK), CHUNK)
        copies.append([])
        for part, (buffer, at, slot, first, groups) in enumerate(PARTS):
            copies[-1].append(
                pltpu.make_async_copy(
                    buffers[buffer].at[pl.ds(at, groups), :, columns],
                    tokens.at[index, pl.ds(first, groups), slot],
                    x_sem.at[index, part],
                )
            )
    for copy in copies[0] + copies[1]:
        copy.start()
    load.wait()
    for index in range(len(near)):
        for copy in copies[index]:
            copy.wait()
        if index + 2 < len(near):
            for copy in copies[index + 2]:
                copy.start()
        weigh(turned, tokens[index].reshape(ROWS, CHUNK), out[index])


def near_shares(order, turned, buffers, near):
    count = len(buffers)
    return pl.pallas_call(
        functools.partial(near_kernel, count, near),
        out_shape=[SHARE] * len(near),
        in_specs=[SMEM] + [HBM] * (1 + count),
        out_specs=[VMEM] * len(near),
        scratch_shapes=[
            pltpu.VMEM((len(near), PATCHES // GROUP, FRAMES, GROUP, CHUNK), jnp.bfloat16),
            pltpu.VMEM((COLS, ROWS), jnp.bfloat16),
            pltpu.SemaphoreType.DMA((1,)),
            pltpu.SemaphoreType.DMA((len(near), len(PARTS))),
        ],
        compiler_params=pltpu.CompilerParams(vmem_limit_bytes=44 * 2**20),
        cost_estimate=pl.CostEstimate(
            flops=2 * ROWS * len(near) * CHUNK * COLS,
            bytes_accessed=2 * ROWS * len(near) * CHUNK,
            transcendentals=0,
        ),
    )(order, turned, *buffers)


def far_shares(order, mask, w, g, buffers):
    count = len(buffers)
    groups = PATCHES // GROUP
    return pl.pallas_call(
        functools.partial(share_kernel, count),
        out_shape=[jax.ShapeDtypeStruct((COLS, ROWS), jnp.bfloat16)] + [SHARE] * len(FAR),
        in_specs=[SMEM, VMEM] + [HBM] * (2 + count),
        out_specs=[HBM] + [VMEM] * len(FAR),
        scratch_shapes=[
            pltpu.VMEM((groups, FRAMES, GROUP, WIDTH), jnp.bfloat16),
            pltpu.VMEM((groups, FRAMES, GROUP, COLS), jnp.bfloat16),
            pltpu.VMEM((groups, FRAMES, GROUP, HEAD_DIM), jnp.bfloat16),
            pltpu.VMEM((COLS, ROWS), jnp.bfloat16),
            pltpu.VMEM((WIDTH, COLS), jnp.bfloat16),
            pltpu.SemaphoreType.DMA((2,)),
            pltpu.SemaphoreType.DMA((len(PARTS),)),
            pltpu.SemaphoreType.DMA((FRAMES,)),
        ],
        compiler_params=pltpu.CompilerParams(vmem_limit_bytes=44 * 2**20),
        cost_estimate=pl.CostEstimate(
            flops=2 * ROWS * WIDTH * COLS, bytes_accessed=2 * ROWS * WIDTH, transcendentals=0
        ),
    )(order, mask, w, g, *buffers)


def add(*parts):
    return sum(part.astype(jnp.float32) for part in parts).astype(jnp.bfloat16)


def local(inputs, grad_attn, w_qkv):
    table = jnp.asarray(tables())[lax.axis_index(AXES)]
    rows_w = take_rows(table[40:41], w_qkv.transpose(1, 0, 2))
    rows_w = lax.ppermute(rows_w, AXES, worker_moves())
    w = lax.all_gather(rows_w, "z", axis=0, tiled=True)
    exchange = lambda value, axes: lax.all_to_all(
        value, axes, split_axis=0, concat_axis=0, tiled=True
    )
    heads_g = exchange(after(grad_attn[0], rows_w).reshape(FRAMES, PATCHES, HEAD_DIM), TOK)
    frames_g = exchange(heads_g, ("core", "x", "yl"))
    steps = gather_frames(inputs[0], (rows_w,), (heads_g,), (frames_g,))
    g = frames_g.reshape(FRAMES, PATCHES // GROUP, GROUP, HEAD_DIM)
    first, second, third = (
        [buffer.reshape(-1, GROUP, WIDTH) for buffer in buffers] for buffers in steps
    )
    order, buffers = table[:24], first + second + third
    turned, far = far_shares(order, visible(table[24:40]), w, g, buffers)
    beside = lax.optimization_barrier
    shares = lambda near: near_shares(order, turned, buffers, near)
    up, down, (share_3, share_5) = beside(
        (shift(far[0], "z", 1), shift(far[1], "z", -1), shares(NEAR_A))
    )
    up = jnp.stack((add(up, share_3[0]), share_3[1]))
    down = jnp.stack((share_5[0], add(down, share_5[1])))
    up, down, near = beside((shift(up, "z", 1), shift(down, "z", -1), shares(NEAR_B)))
    for step in (0, 2):
        up = shift(add(up, near[step]), "z", 1)
        down = shift(add(down, near[step + 1]), "z", -1)
    mine = add(up, down, near[4])
    yh = lax.axis_index("yh")
    total = None
    for flip in range(2):
        part = lax.dynamic_index_in_dim(mine, (yh + flip) % 2, 0, keepdims=False)
        part = lax.ppermute(part, AXES, plane_moves(flip)).astype(jnp.float32)
        total = part if total is None else total + part
    return lax.ppermute(total.astype(jnp.bfloat16), AXES, line_moves()).transpose(1, 0, 2)


def solution(mesh):
    fine = Mesh(mesh.devices.reshape(SIZES), AXES)
    in_specs = (P(FRAME, TOK, None), P(FRAME, None, TOK), P(None, None, TOK))
    out_specs = P(FRAME, None, TOK)
    return jax.shard_map(local, mesh=fine, in_specs=in_specs, out_specs=out_specs, check_vma=False)
```

```python
import functools
import math

import jax
import jax.numpy as jnp
import numpy as np
from jax import lax
from jax.experimental import pallas as pl
from jax.experimental.pallas import tpu as pltpu
from jax.sharding import Mesh, PartitionSpec as P

HEAD_DIM = 128
AXES = ("yl", "x", "core", "yh", "z")
SIZES = (2, 4, 2, 2, 8)
FRAME = AXES[:3]
TOK = AXES[3:]
FRAMES = 16
PATCHES = 128
CUT_A, CUT_B = 48, 96
CUTS = ((0, CUT_A), (CUT_A, CUT_B), (CUT_B, PATCHES))
STEP = 4
FAR = (4,)
NEAR_A = (3, 5)
NEAR_B = (2, 6, 1, 7, 0)
CUT_FLOPS = 2 * 10**10
WIDTH = 4096
COLS = 3 * HEAD_DIM
ROWS = FRAMES * PATCHES
GROUP = 16
CHUNK = WIDTH // 8
SHARE = jax.ShapeDtypeStruct((2, 3, CHUNK // 2, HEAD_DIM), jnp.bfloat16)

SAME_CORE = ((0, 0), (0, 1), (0, -1), (1, 0), (0, 2), (1, 1), (1, -1), (1, 2))
SLOTS = [(dy, dx, dc) for dy, dx in SAME_CORE for dc in (0, 1)]


def device(yl, x, core, yh, z):
    place = 0
    for value, size in zip((yl, x, core, yh, z), SIZES):
        place = place * size + value % size
    return place


def worker_moves():
    pairs = []
    for yl, x, core, yh, z in np.ndindex(*SIZES):
        owner = device(yl ^ (z % 2), x + z // 2, yh, core, 2 * x + yl)
        pairs.append((owner, device(yl, x, core, yh, z)))
    return pairs


def plane_moves(flip):
    pairs = []
    for yl, x, core, yh, z in np.ndindex(*SIZES):
        target = device(yl ^ (z % 2), x + z // 2, yh ^ flip, core, z)
        pairs.append((device(yl, x, core, yh, z), target))
    return pairs


def line_moves():
    pairs = []
    for yl, x, core, yh, z in np.ndindex(*SIZES):
        target = device(yl, x, core, yh, 2 * ((x - z // 2) % 4) + (yl ^ (z % 2)))
        pairs.append((device(yl, x, core, yh, z), target))
    return pairs


def shift(value, axis, by):
    count = SIZES[AXES.index(axis)]
    return lax.ppermute(value, axis, [(i, (i + by) % count) for i in range(count)])


def after(values, *others):
    return lax.optimization_barrier((values, *others))[0]


def cut_kernel(*refs):
    sems = refs[-1]
    copies = []
    for index, (first, last) in enumerate(CUTS):
        source, target = refs[index], refs[3 + index]
        copies.append(
            pltpu.make_async_copy(source.at[pl.ds(first, last - first)], target, sems.at[index])
        )
        copies[-1].start()
    for copy in copies:
        copy.wait()


def cut(*buffers):
    hbm = pl.BlockSpec(memory_space=pltpu.HBM)
    return pl.pallas_call(
        cut_kernel,
        out_shape=[
            jax.ShapeDtypeStruct((last - first, WIDTH), jnp.bfloat16) for first, last in CUTS
        ],
        in_specs=[hbm] * 3,
        out_specs=[pl.BlockSpec(memory_space=pltpu.VMEM)] * 3,
        scratch_shapes=[pltpu.SemaphoreType.DMA((3,))],
        cost_estimate=pl.CostEstimate(flops=CUT_FLOPS, bytes_accessed=0, transcendentals=0),
    )(*buffers)


def gather_frames(own, early, middle, late, beside_third):
    twin = lambda values: [shift(value, "core", 1) for value in values]
    first = [shift(own, "x", 1), shift(own, "x", -1), shift(own, "yl", 1)]
    own_twin = shift(own, "core", 1)
    left, right, other = after(first, *early)
    second = [shift(other, "x", 1), shift(right, "x", -1), shift(right, "yl", 1)]
    first_twins = twin([left, right, other])
    other_left, far, other_right = after(second, *middle)
    cuts = cut(other_left, other_right, far)
    third = [shift(cuts[0], "x", 1), shift(cuts[1], "x", -1), shift(cuts[2], "yl", 1)]
    second_twins = twin([other_left, far, other_right])
    whole = [own, own_twin, left, right, other, *first_twins]
    whole += [other_left, far, other_right, *second_twins]
    result = beside_third(whole)
    third = after(third, result, *late)
    return whole, [*third, *twin(third)], result


FIRST = [[(slot, 0, PATCHES)] for slot in (0, 1, 4, 2, 6, 5, 3, 7)]
SECOND = [[(slot, 0, PATCHES)] for slot in (12, 8, 10, 13, 9, 11)]
THIRD = [
    [(14 + core, first, last - first)]
    for core in (0, 1)
    for first, last in CUTS
]


def parts_of(places):
    out = []
    for buffer, parts in enumerate(places):
        row = 0
        for slot, first, rows in parts:
            out.append((buffer, row // GROUP, slot, first // GROUP, rows // GROUP))
            row += rows
    return out


PARTS = parts_of(FIRST + SECOND + THIRD)


def tables():
    out = np.zeros((256, 48), np.int32)
    for yl, x, core, yh, z in np.ndindex(*SIZES):
        row = out[device(yl, x, core, yh, z)]
        for slot, (dy, dx, dc) in enumerate(SLOTS):
            row[slot] = (core ^ dc) * 8 + (x + dx) % 4 * 2 + (yl ^ dy)
            row[24 + slot] = ((yl ^ dy) * 4 + (x + dx) % 4) * 2 + (core ^ dc)
        for k in range(8):
            at = (z + k) % 8
            row[16 + k] = (yl ^ (at % 2)) * 4 + (x + at // 2) % 4
        row[40] = (x - z // 2) % 4 * 2 + (yl ^ (z % 2))
    return out


def visible(ids):
    frame = jnp.repeat(ids, GROUP)
    patch = jnp.tile(jnp.arange(GROUP, dtype=jnp.int32), FRAMES)
    allowed = (frame[None, :] <= frame[:, None]) & (patch[None, :] == patch[:, None])
    return allowed.astype(jnp.float32)


VMEM = pl.BlockSpec(memory_space=pltpu.VMEM)
SMEM = pl.BlockSpec(memory_space=pltpu.SMEM)
HBM = pl.BlockSpec(memory_space=pltpu.HBM)


def take_kernel(start, w_ref, out, sem):
    copies = []
    for j in range(3):
        rows = pl.ds(pl.multiple_of(start[0] * CHUNK, CHUNK), CHUNK)
        columns = pl.ds(j * HEAD_DIM, HEAD_DIM)
        copies.append(pltpu.make_async_copy(w_ref.at[j, rows], out.at[:, columns], sem.at[j]))
        copies[-1].start()
    for copy in copies:
        copy.wait()


def take_rows(start, w):
    return pl.pallas_call(
        take_kernel,
        out_shape=jax.ShapeDtypeStruct((CHUNK, COLS), jnp.bfloat16),
        in_specs=[SMEM, HBM],
        out_specs=VMEM,
        scratch_shapes=[pltpu.SemaphoreType.DMA((3,))],
    )(start, w)


def attend(proj, grads, mask, turned):
    factor = 1.0 / math.sqrt(HEAD_DIM)
    size = FRAMES * GROUP

    def body(step, carry):
        part = proj[step].reshape(size, COLS)
        query, key, value = (part[:, j * HEAD_DIM : (j + 1) * HEAD_DIM] for j in range(3))
        grad = grads[step].reshape(size, HEAD_DIM)
        across = (((1,), (1,)), ((), ()))
        down = (((0,), (0,)), ((), ()))
        dot = functools.partial(lax.dot_general, preferred_element_type=jnp.float32)
        scores = dot(query, key, across) * factor
        scores = jnp.where(mask[...] > 0.5, scores, -1e30)
        exponent = jnp.exp(scores - jnp.max(scores, axis=-1, keepdims=True))
        probs = exponent / jnp.sum(exponent, axis=-1, keepdims=True)
        grad_probs = dot(grad, value, across)
        row_dot = jnp.sum(grad_probs * probs, axis=-1, keepdims=True)
        grad_scores = (probs * (grad_probs - row_dot)).astype(jnp.bfloat16)
        probs_b = probs.astype(jnp.bfloat16)
        grad_query = jnp.dot(grad_scores, key, preferred_element_type=jnp.float32) * factor
        grad_key = dot(grad_scores, query, down) * factor
        grad_value = dot(probs_b, grad, down)
        columns = pl.ds(pl.multiple_of(step * size, size), size)
        for j, result in enumerate((grad_query, grad_key, grad_value)):
            turned[j * HEAD_DIM : (j + 1) * HEAD_DIM, columns] = result.T.astype(jnp.bfloat16)
        return carry

    lax.fori_loop(0, PATCHES // GROUP, body, 0, unroll=4)


def project_kernel(count, w_ref, *refs):
    buffers, out = refs[:count], refs[count]
    tokens, result, w, w_sem, x_sem, o_sem = refs[count + 1 :]
    groups = PATCHES // GROUP
    weights = pltpu.make_async_copy(w_ref, w, w_sem.at[0])
    copies = []
    for index, ref in enumerate(buffers):
        rows = pl.ds(index * groups, groups)
        copies.append(pltpu.make_async_copy(ref, tokens.at[rows], x_sem.at[index]))
    steps = [copies[at : at + STEP] for at in range(0, count, STEP)]
    weights.start()
    for copy in steps[0]:
        copy.start()
    weights.wait()
    stores = []
    for step, here in enumerate(steps):
        for copy in here:
            copy.wait()
        for copy in steps[step + 1] if step + 1 < len(steps) else ():
            copy.start()
        rows = pl.ds(step * STEP * groups, len(here) * groups)
        value = tokens[rows].reshape(len(here) * PATCHES, WIDTH)
        value = jnp.dot(value, w[...], preferred_element_type=jnp.float32)
        result[rows] = value.astype(jnp.bfloat16).reshape(-1, GROUP, COLS)
        stores.append(pltpu.make_async_copy(result.at[rows], out.at[rows], o_sem.at[step]))
        stores[-1].start()
    for store in stores:
        store.wait()


def project(w, buffers):
    count = len(buffers)
    groups = count * PATCHES // GROUP
    return pl.pallas_call(
        functools.partial(project_kernel, count),
        out_shape=jax.ShapeDtypeStruct((groups, GROUP, COLS), jnp.bfloat16),
        in_specs=[HBM] * (1 + count),
        out_specs=HBM,
        scratch_shapes=[
            pltpu.VMEM((groups, GROUP, WIDTH), jnp.bfloat16),
            pltpu.VMEM((groups, GROUP, COLS), jnp.bfloat16),
            pltpu.VMEM((WIDTH, COLS), jnp.bfloat16),
            pltpu.SemaphoreType.DMA((1,)),
            pltpu.SemaphoreType.DMA((count,)),
            pltpu.SemaphoreType.DMA((count,)),
        ],
        compiler_params=pltpu.CompilerParams(vmem_limit_bytes=48 * 2**20),
        cost_estimate=pl.CostEstimate(
            flops=2 * groups * GROUP * WIDTH * COLS,
            bytes_accessed=2 * groups * GROUP * WIDTH,
            transcendentals=0,
        ),
    )(w, *buffers)


def share_kernel(count, order, mask, w_ref, g_ref, early, *refs):
    buffers, turned_out, out = refs[:count], refs[count], refs[count + 1 : count + 1 + len(FAR)]
    tokens, proj, grads, turned, w, w_sem, x_sem, g_sem, p_sem = refs[count + 1 + len(FAR) :]
    copies = []
    for index, (buffer, at, slot, first, groups) in enumerate(PARTS):
        copies.append(
            pltpu.make_async_copy(
                buffers[buffer].at[pl.ds(at, groups)],
                tokens.at[pl.ds(first, groups), slot],
                x_sem.at[index],
            )
        )
    copies, last = copies[: -len(THIRD)], copies[-len(THIRD) :]
    small = []
    for slot in range(FRAMES):
        small.append(
            pltpu.make_async_copy(g_ref.at[order[slot]], grads.at[:, slot], g_sem.at[slot])
        )
    for index, (buffer, _, slot, _, groups) in enumerate(parts_of(FIRST + SECOND)):
        source = early.at[pl.ds(buffer * groups, groups)]
        small.append(pltpu.make_async_copy(source, proj.at[:, slot], p_sem.at[index]))
    weights = pltpu.make_async_copy(w_ref, w, w_sem.at[0])
    for copy in [weights] + last + small:
        copy.start()
    for copy in [weights] + last:
        copy.wait()
    for copy in copies:
        copy.start()
    rows = tokens[:, FRAMES - 2 :].reshape(2 * PATCHES, WIDTH)
    result = jnp.dot(rows, w[...], preferred_element_type=jnp.float32)
    proj[:, FRAMES - 2 :] = result.astype(jnp.bfloat16).reshape(-1, 2, GROUP, COLS)
    for copy in small:
        copy.wait()
    attend(proj, grads, mask, turned)
    store = pltpu.make_async_copy(turned, turned_out, w_sem.at[1])
    store.start()
    for copy in copies:
        copy.wait()
    for index, ahead in enumerate(FAR):
        columns = pl.ds(pl.multiple_of(order[16 + ahead] * CHUNK, CHUNK), CHUNK)
        rows = tokens[:, :, :, columns].reshape(ROWS, CHUNK)
        weigh(turned, rows, out[index])
    store.wait()


def weigh(turned, rows, out):
    value = jnp.dot(turned[...], rows, preferred_element_type=jnp.float32)
    for half in range(2):
        rows = slice(half * CHUNK // 2, (half + 1) * CHUNK // 2)
        for j in range(3):
            part = value[j * HEAD_DIM : (j + 1) * HEAD_DIM, rows]
            out[half, j] = part.T.astype(jnp.bfloat16)


def near_kernel(count, near, order, turned_ref, *refs):
    buffers, out = refs[:count], refs[count : count + len(near)]
    tokens, turned, t_sem, x_sem = refs[count + len(near) :]
    load = pltpu.make_async_copy(turned_ref, turned, t_sem.at[0])
    load.start()
    copies = []
    for index, ahead in enumerate(near):
        columns = pl.ds(pl.multiple_of(order[16 + ahead] * CHUNK, CHUNK), CHUNK)
        copies.append([])
        for part, (buffer, at, slot, first, groups) in enumerate(PARTS):
            copies[-1].append(
                pltpu.make_async_copy(
                    buffers[buffer].at[pl.ds(at, groups), :, columns],
                    tokens.at[index, pl.ds(first, groups), slot],
                    x_sem.at[index, part],
                )
            )
    for copy in copies[0] + copies[1]:
        copy.start()
    load.wait()
    for index in range(len(near)):
        for copy in copies[index]:
            copy.wait()
        if index + 2 < len(near):
            for copy in copies[index + 2]:
                copy.start()
        weigh(turned, tokens[index].reshape(ROWS, CHUNK), out[index])


def near_shares(order, turned, buffers, near):
    count = len(buffers)
    return pl.pallas_call(
        functools.partial(near_kernel, count, near),
        out_shape=[SHARE] * len(near),
        in_specs=[SMEM] + [HBM] * (1 + count),
        out_specs=[VMEM] * len(near),
        scratch_shapes=[
            pltpu.VMEM((len(near), PATCHES // GROUP, FRAMES, GROUP, CHUNK), jnp.bfloat16),
            pltpu.VMEM((COLS, ROWS), jnp.bfloat16),
            pltpu.SemaphoreType.DMA((1,)),
            pltpu.SemaphoreType.DMA((len(near), len(PARTS))),
        ],
        compiler_params=pltpu.CompilerParams(vmem_limit_bytes=48 * 2**20),
        cost_estimate=pl.CostEstimate(
            flops=2 * ROWS * len(near) * CHUNK * COLS,
            bytes_accessed=2 * ROWS * len(near) * CHUNK,
            transcendentals=0,
        ),
    )(order, turned, *buffers)


def far_shares(order, mask, w, g, early, buffers):
    count = len(buffers)
    groups = PATCHES // GROUP
    return pl.pallas_call(
        functools.partial(share_kernel, count),
        out_shape=[jax.ShapeDtypeStruct((COLS, ROWS), jnp.bfloat16)] + [SHARE] * len(FAR),
        in_specs=[SMEM, VMEM] + [HBM] * (3 + count),
        out_specs=[HBM] + [VMEM] * len(FAR),
        scratch_shapes=[
            pltpu.VMEM((groups, FRAMES, GROUP, WIDTH), jnp.bfloat16),
            pltpu.VMEM((groups, FRAMES, GROUP, COLS), jnp.bfloat16),
            pltpu.VMEM((groups, FRAMES, GROUP, HEAD_DIM), jnp.bfloat16),
            pltpu.VMEM((COLS, ROWS), jnp.bfloat16),
            pltpu.VMEM((WIDTH, COLS), jnp.bfloat16),
            pltpu.SemaphoreType.DMA((2,)),
            pltpu.SemaphoreType.DMA((len(PARTS),)),
            pltpu.SemaphoreType.DMA((FRAMES,)),
            pltpu.SemaphoreType.DMA((len(FIRST + SECOND),)),
        ],
        compiler_params=pltpu.CompilerParams(vmem_limit_bytes=48 * 2**20),
        cost_estimate=pl.CostEstimate(
            flops=2 * ROWS * WIDTH * COLS, bytes_accessed=2 * ROWS * WIDTH, transcendentals=0
        ),
    )(order, mask, w, g, early, *buffers)


def add(*parts):
    return sum(part.astype(jnp.float32) for part in parts).astype(jnp.bfloat16)


def local(inputs, grad_attn, w_qkv):
    table = jnp.asarray(tables())[lax.axis_index(AXES)]
    rows_w = take_rows(table[40:41], w_qkv.transpose(1, 0, 2))
    rows_w = lax.ppermute(rows_w, AXES, worker_moves())
    w = lax.all_gather(rows_w, "z", axis=0, tiled=True)
    exchange = lambda value, axes: lax.all_to_all(
        value, axes, split_axis=0, concat_axis=0, tiled=True
    )
    heads_g = exchange(after(grad_attn[0], rows_w).reshape(FRAMES, PATCHES, HEAD_DIM), TOK)
    frames_g = exchange(heads_g, ("core", "x", "yl"))
    grouped = lambda buffers: [buffer.reshape(-1, GROUP, WIDTH) for buffer in buffers]
    whole, third, early = gather_frames(
        inputs[0], (rows_w,), (heads_g,), (frames_g,), lambda whole: project(w, grouped(whole))
    )
    g = frames_g.reshape(FRAMES, PATCHES // GROUP, GROUP, HEAD_DIM)
    order, buffers = table[:24], grouped(whole + third)
    turned, far = far_shares(order, visible(table[24:40]), w, g, early, buffers)
    beside = lax.optimization_barrier
    shares = lambda near: near_shares(order, turned, buffers, near)
    up, down, (share_3, share_5) = beside(
        (shift(far[0], "z", 1), shift(far[1], "z", -1), shares(NEAR_A))
    )
    up = jnp.stack((add(up, share_3[0]), share_3[1]))
    down = jnp.stack((share_5[0], add(down, share_5[1])))
    up, down, near = beside((shift(up, "z", 1), shift(down, "z", -1), shares(NEAR_B)))
    for step in (0, 2):
        up = shift(add(up, near[step]), "z", 1)
        down = shift(add(down, near[step + 1]), "z", -1)
    mine = add(up, down, near[4])
    yh = lax.axis_index("yh")
    total = None
    for flip in range(2):
        part = lax.dynamic_index_in_dim(mine, (yh + flip) % 2, 0, keepdims=False)
        part = lax.ppermute(part, AXES, plane_moves(flip)).astype(jnp.float32)
        total = part if total is None else total + part
    return lax.ppermute(total.astype(jnp.bfloat16), AXES, line_moves()).transpose(1, 0, 2)


def solution(mesh):
    fine = Mesh(mesh.devices.reshape(SIZES), AXES)
    in_specs = (P(FRAME, TOK, None), P(FRAME, None, TOK), P(None, None, TOK))
    out_specs = P(FRAME, None, TOK)
    return jax.shard_map(local, mesh=fine, in_specs=in_specs, out_specs=out_specs, check_vma=False)
```

```python
import functools
import math

import jax
import jax.numpy as jnp
import numpy as np
from jax import lax
from jax.experimental import pallas as pl
from jax.experimental.pallas import tpu as pltpu
from jax.sharding import Mesh, PartitionSpec as P

HEAD_DIM = 128
AXES = ("yl", "x", "core", "yh", "z")
SIZES = (2, 4, 2, 2, 8)
FRAME = AXES[:3]
TOK = AXES[3:]
FRAMES = 16
PATCHES = 128
CUT_A, CUT_B = 48, 96
CUTS = ((0, CUT_A), (CUT_A, CUT_B), (CUT_B, PATCHES))
STEP = 4
FAR = (4,)
NEAR = ((3, 5), (2, 6), (1, 7, 0))
CUT_FLOPS = 3 * 10**10
WIDTH = 4096
COLS = 3 * HEAD_DIM
ROWS = FRAMES * PATCHES
GROUP = 16
CHUNK = WIDTH // 8
SHARE = jax.ShapeDtypeStruct((2, 3, CHUNK // 2, HEAD_DIM), jnp.bfloat16)

SAME_CORE = ((0, 0), (0, 1), (0, -1), (1, 0), (0, 2), (1, 1), (1, -1), (1, 2))
SLOTS = [(dy, dx, dc) for dy, dx in SAME_CORE for dc in (0, 1)]


def device(yl, x, core, yh, z):
    place = 0
    for value, size in zip((yl, x, core, yh, z), SIZES):
        place = place * size + value % size
    return place


def worker_moves():
    pairs = []
    for yl, x, core, yh, z in np.ndindex(*SIZES):
        owner = device(yl ^ (z % 2), x + z // 2, yh, core, 2 * x + yl)
        pairs.append((owner, device(yl, x, core, yh, z)))
    return pairs


def plane_moves(flip):
    pairs = []
    for yl, x, core, yh, z in np.ndindex(*SIZES):
        target = device(yl ^ (z % 2), x + z // 2, yh ^ flip, core, z)
        pairs.append((device(yl, x, core, yh, z), target))
    return pairs


def line_moves():
    pairs = []
    for yl, x, core, yh, z in np.ndindex(*SIZES):
        target = device(yl, x, core, yh, 2 * ((x - z // 2) % 4) + (yl ^ (z % 2)))
        pairs.append((device(yl, x, core, yh, z), target))
    return pairs


def shift(value, axis, by):
    count = SIZES[AXES.index(axis)]
    return lax.ppermute(value, axis, [(i, (i + by) % count) for i in range(count)])


def after(values, *others):
    return lax.optimization_barrier((values, *others))[0]


def cut_kernel(*refs):
    sems = refs[-1]
    copies = []
    for index, (first, last) in enumerate(CUTS):
        source, target = refs[index], refs[3 + index]
        copies.append(
            pltpu.make_async_copy(source.at[pl.ds(first, last - first)], target, sems.at[index])
        )
        copies[-1].start()
    for copy in copies:
        copy.wait()


def cut(*buffers):
    hbm = pl.BlockSpec(memory_space=pltpu.HBM)
    return pl.pallas_call(
        cut_kernel,
        out_shape=[
            jax.ShapeDtypeStruct((last - first, WIDTH), jnp.bfloat16) for first, last in CUTS
        ],
        in_specs=[hbm] * 3,
        out_specs=[pl.BlockSpec(memory_space=pltpu.VMEM)] * 3,
        scratch_shapes=[pltpu.SemaphoreType.DMA((3,))],
        cost_estimate=pl.CostEstimate(flops=CUT_FLOPS, bytes_accessed=0, transcendentals=0),
    )(*buffers)


def gather_frames(own, early, middle, late):
    twin = lambda values: [shift(value, "core", 1) for value in values]
    first = [shift(own, "x", 1), shift(own, "x", -1), shift(own, "yl", 1)]
    own_twin = shift(own, "core", 1)
    left, right, other = after(first, *early)
    second = [shift(other, "x", 1), shift(right, "x", -1), shift(right, "yl", 1)]
    first_twins = twin([left, right, other])
    other_left, far, other_right = after(second, *middle)
    cuts = cut(other_left, other_right, far)
    third = [shift(cuts[0], "x", 1), shift(cuts[1], "x", -1), shift(cuts[2], "yl", 1)]
    second_twins = twin([other_left, far, other_right])
    third = after(third, *late)
    return (
        [own, own_twin, left, right, other, *first_twins],
        [other_left, far, other_right, *second_twins],
        [*third, *twin(third)],
    )


FIRST = [[(slot, 0, PATCHES)] for slot in (0, 1, 4, 2, 6, 5, 3, 7)]
SECOND = [[(slot, 0, PATCHES)] for slot in (12, 8, 10, 13, 9, 11)]
THIRD = [
    [(14 + core, first, last - first)]
    for core in (0, 1)
    for first, last in CUTS
]


def parts_of(places):
    out = []
    for buffer, parts in enumerate(places):
        row = 0
        for slot, first, rows in parts:
            out.append((buffer, row // GROUP, slot, first // GROUP, rows // GROUP))
            row += rows
    return out


PARTS = parts_of(FIRST + SECOND + THIRD)


def tables():
    out = np.zeros((256, 48), np.int32)
    for yl, x, core, yh, z in np.ndindex(*SIZES):
        row = out[device(yl, x, core, yh, z)]
        for slot, (dy, dx, dc) in enumerate(SLOTS):
            row[slot] = (core ^ dc) * 8 + (x + dx) % 4 * 2 + (yl ^ dy)
            row[24 + slot] = ((yl ^ dy) * 4 + (x + dx) % 4) * 2 + (core ^ dc)
        for k in range(8):
            at = (z + k) % 8
            row[16 + k] = (yl ^ (at % 2)) * 4 + (x + at // 2) % 4
        row[40] = (x - z // 2) % 4 * 2 + (yl ^ (z % 2))
    return out


def visible(ids):
    frame = jnp.repeat(ids, GROUP)
    patch = jnp.tile(jnp.arange(GROUP, dtype=jnp.int32), FRAMES)
    allowed = (frame[None, :] <= frame[:, None]) & (patch[None, :] == patch[:, None])
    return allowed.astype(jnp.float32)


VMEM = pl.BlockSpec(memory_space=pltpu.VMEM)
SMEM = pl.BlockSpec(memory_space=pltpu.SMEM)
HBM = pl.BlockSpec(memory_space=pltpu.HBM)


def take_kernel(start, w_ref, out, sem):
    copies = []
    for j in range(3):
        rows = pl.ds(pl.multiple_of(start[0] * CHUNK, CHUNK), CHUNK)
        columns = pl.ds(j * HEAD_DIM, HEAD_DIM)
        copies.append(pltpu.make_async_copy(w_ref.at[j, rows], out.at[:, columns], sem.at[j]))
        copies[-1].start()
    for copy in copies:
        copy.wait()


def take_rows(start, w):
    return pl.pallas_call(
        take_kernel,
        out_shape=jax.ShapeDtypeStruct((CHUNK, COLS), jnp.bfloat16),
        in_specs=[SMEM, HBM],
        out_specs=VMEM,
        scratch_shapes=[pltpu.SemaphoreType.DMA((3,))],
    )(start, w)


def attend(proj, grads, mask, turned):
    factor = 1.0 / math.sqrt(HEAD_DIM)
    size = FRAMES * GROUP

    def body(step, carry):
        part = proj[step].reshape(size, COLS)
        query, key, value = (part[:, j * HEAD_DIM : (j + 1) * HEAD_DIM] for j in range(3))
        grad = grads[step].reshape(size, HEAD_DIM)
        across = (((1,), (1,)), ((), ()))
        down = (((0,), (0,)), ((), ()))
        dot = functools.partial(lax.dot_general, preferred_element_type=jnp.float32)
        scores = dot(query, key, across) * factor
        scores = jnp.where(mask[...] > 0.5, scores, -1e30)
        exponent = jnp.exp(scores - jnp.max(scores, axis=-1, keepdims=True))
        probs = exponent / jnp.sum(exponent, axis=-1, keepdims=True)
        grad_probs = dot(grad, value, across)
        row_dot = jnp.sum(grad_probs * probs, axis=-1, keepdims=True)
        grad_scores = (probs * (grad_probs - row_dot)).astype(jnp.bfloat16)
        probs_b = probs.astype(jnp.bfloat16)
        grad_query = jnp.dot(grad_scores, key, preferred_element_type=jnp.float32) * factor
        grad_key = dot(grad_scores, query, down) * factor
        grad_value = dot(probs_b, grad, down)
        columns = pl.ds(pl.multiple_of(step * size, size), size)
        for j, result in enumerate((grad_query, grad_key, grad_value)):
            turned[j * HEAD_DIM : (j + 1) * HEAD_DIM, columns] = result.T.astype(jnp.bfloat16)
        return carry

    lax.fori_loop(0, PATCHES // GROUP, body, 0, unroll=4)


def share_kernel(count, order, mask, w_ref, g_ref, *refs):
    buffers, turned_out, out = refs[:count], refs[count], refs[count + 1 : count + 1 + len(FAR)]
    tokens, proj, grads, turned, w, w_sem, x_sem, g_sem = refs[count + 1 + len(FAR) :]
    arrivals = [[] for _ in range(FRAMES)]
    for index, (buffer, at, slot, first, groups) in enumerate(PARTS):
        arrivals[slot].append(
            pltpu.make_async_copy(
                buffers[buffer].at[pl.ds(at, groups)],
                tokens.at[pl.ds(first, groups), slot],
                x_sem.at[index],
            )
        )
    cotangents = []
    for slot in range(FRAMES):
        cotangents.append(
            pltpu.make_async_copy(g_ref.at[order[slot]], grads.at[:, slot], g_sem.at[slot])
        )
    weights = pltpu.make_async_copy(w_ref, w, w_sem.at[0])

    def step_copies(step):
        return [copy for slot in range(STEP * step, STEP * step + STEP) for copy in arrivals[slot]]

    weights.start()
    for copy in step_copies(0):
        copy.start()
    weights.wait()
    steps = FRAMES // STEP
    for step in range(steps):
        for copy in step_copies(step):
            copy.wait()
        for copy in step_copies(step + 1) if step + 1 < steps else cotangents:
            copy.start()
        slots = slice(STEP * step, STEP * step + STEP)
        rows = tokens[:, slots].reshape(STEP * PATCHES, WIDTH)
        result = jnp.dot(rows, w[...], preferred_element_type=jnp.float32)
        proj[:, slots] = result.astype(jnp.bfloat16).reshape(-1, STEP, GROUP, COLS)
    for copy in cotangents:
        copy.wait()
    attend(proj, grads, mask, turned)
    store = pltpu.make_async_copy(turned, turned_out, w_sem.at[1])
    store.start()
    for index, ahead in enumerate(FAR):
        columns = pl.ds(pl.multiple_of(order[16 + ahead] * CHUNK, CHUNK), CHUNK)
        rows = tokens[:, :, :, columns].reshape(ROWS, CHUNK)
        weigh(turned, rows, out[index])
    store.wait()


def weigh(turned, rows, out):
    value = jnp.dot(turned[...], rows, preferred_element_type=jnp.float32)
    for half in range(2):
        rows = slice(half * CHUNK // 2, (half + 1) * CHUNK // 2)
        for j in range(3):
            part = value[j * HEAD_DIM : (j + 1) * HEAD_DIM, rows]
            out[half, j] = part.T.astype(jnp.bfloat16)


def near_kernel(count, near, order, turned_ref, *refs):
    buffers, out = refs[:count], refs[count : count + len(near)]
    tokens, turned, t_sem, x_sem = refs[count + len(near) :]
    load = pltpu.make_async_copy(turned_ref, turned, t_sem.at[0])
    load.start()
    copies = []
    for index, ahead in enumerate(near):
        columns = pl.ds(pl.multiple_of(order[16 + ahead] * CHUNK, CHUNK), CHUNK)
        copies.append([])
        for part, (buffer, at, slot, first, groups) in enumerate(PARTS):
            copies[-1].append(
                pltpu.make_async_copy(
                    buffers[buffer].at[pl.ds(at, groups), :, columns],
                    tokens.at[index, pl.ds(first, groups), slot],
                    x_sem.at[index, part],
                )
            )
    for copy in copies[0] + copies[1]:
        copy.start()
    load.wait()
    for index in range(len(near)):
        for copy in copies[index]:
            copy.wait()
        if index + 2 < len(near):
            for copy in copies[index + 2]:
                copy.start()
        weigh(turned, tokens[index].reshape(ROWS, CHUNK), out[index])


def near_shares(order, turned, buffers, near):
    count = len(buffers)
    return pl.pallas_call(
        functools.partial(near_kernel, count, near),
        out_shape=[SHARE] * len(near),
        in_specs=[SMEM] + [HBM] * (1 + count),
        out_specs=[VMEM] * len(near),
        scratch_shapes=[
            pltpu.VMEM((len(near), PATCHES // GROUP, FRAMES, GROUP, CHUNK), jnp.bfloat16),
            pltpu.VMEM((COLS, ROWS), jnp.bfloat16),
            pltpu.SemaphoreType.DMA((1,)),
            pltpu.SemaphoreType.DMA((len(near), len(PARTS))),
        ],
        compiler_params=pltpu.CompilerParams(vmem_limit_bytes=48 * 2**20),
        cost_estimate=pl.CostEstimate(
            flops=2 * ROWS * len(near) * CHUNK * COLS,
            bytes_accessed=2 * ROWS * len(near) * CHUNK,
            transcendentals=0,
        ),
    )(order, turned, *buffers)


def far_shares(order, mask, w, g, buffers):
    count = len(buffers)
    groups = PATCHES // GROUP
    return pl.pallas_call(
        functools.partial(share_kernel, count),
        out_shape=[jax.ShapeDtypeStruct((COLS, ROWS), jnp.bfloat16)] + [SHARE] * len(FAR),
        in_specs=[SMEM, VMEM] + [HBM] * (2 + count),
        out_specs=[HBM] + [VMEM] * len(FAR),
        scratch_shapes=[
            pltpu.VMEM((groups, FRAMES, GROUP, WIDTH), jnp.bfloat16),
            pltpu.VMEM((groups, FRAMES, GROUP, COLS), jnp.bfloat16),
            pltpu.VMEM((groups, FRAMES, GROUP, HEAD_DIM), jnp.bfloat16),
            pltpu.VMEM((COLS, ROWS), jnp.bfloat16),
            pltpu.VMEM((WIDTH, COLS), jnp.bfloat16),
            pltpu.SemaphoreType.DMA((2,)),
            pltpu.SemaphoreType.DMA((len(PARTS),)),
            pltpu.SemaphoreType.DMA((FRAMES,)),
        ],
        compiler_params=pltpu.CompilerParams(vmem_limit_bytes=48 * 2**20),
        cost_estimate=pl.CostEstimate(
            flops=2 * ROWS * WIDTH * COLS, bytes_accessed=2 * ROWS * WIDTH, transcendentals=0
        ),
    )(order, mask, w, g, *buffers)


def add(*parts):
    return sum(part.astype(jnp.float32) for part in parts).astype(jnp.bfloat16)


def local(inputs, grad_attn, w_qkv):
    table = jnp.asarray(tables())[lax.axis_index(AXES)]
    rows_w = take_rows(table[40:41], w_qkv.transpose(1, 0, 2))
    rows_w = lax.ppermute(rows_w, AXES, worker_moves())
    w = lax.all_gather(rows_w, "z", axis=0, tiled=True)
    exchange = lambda value, axes: lax.all_to_all(
        value, axes, split_axis=0, concat_axis=0, tiled=True
    )
    heads_g = exchange(after(grad_attn[0], rows_w).reshape(FRAMES, PATCHES, HEAD_DIM), TOK)
    frames_g = exchange(heads_g, ("core", "x", "yl"))
    steps = gather_frames(inputs[0], (rows_w,), (heads_g,), (frames_g,))
    g = frames_g.reshape(FRAMES, PATCHES // GROUP, GROUP, HEAD_DIM)
    first, second, third = (
        [buffer.reshape(-1, GROUP, WIDTH) for buffer in buffers] for buffers in steps
    )
    order, buffers = table[:24], first + second + third
    turned, far = far_shares(order, visible(table[24:40]), w, g, buffers)
    beside = lax.optimization_barrier
    shares = lambda near: near_shares(order, turned, buffers, near)
    up, down, near = beside((shift(far[0], "z", 1), shift(far[1], "z", -1), shares(NEAR[0])))
    up = jnp.stack((add(up, near[0][0]), near[0][1]))
    down = jnp.stack((near[1][0], add(down, near[1][1])))
    for step in NEAR[1:]:
        up, down, near = beside((shift(up, "z", 1), shift(down, "z", -1), shares(step)))
        up, down = add(up, near[0]), add(down, near[1])
    mine = add(shift(up, "z", 1), shift(down, "z", -1), near[2])
    yh = lax.axis_index("yh")
    total = None
    for flip in range(2):
        part = lax.dynamic_index_in_dim(mine, (yh + flip) % 2, 0, keepdims=False)
        part = lax.ppermute(part, AXES, plane_moves(flip)).astype(jnp.float32)
        total = part if total is None else total + part
    return lax.ppermute(total.astype(jnp.bfloat16), AXES, line_moves()).transpose(1, 0, 2)


def solution(mesh):
    fine = Mesh(mesh.devices.reshape(SIZES), AXES)
    in_specs = (P(FRAME, TOK, None), P(FRAME, None, TOK), P(None, None, TOK))
    out_specs = P(FRAME, None, TOK)
    return jax.shard_map(local, mesh=fine, in_specs=in_specs, out_specs=out_specs, check_vma=False)
```

```python
import functools
import math

import jax
import jax.numpy as jnp
import numpy as np
from jax import lax
from jax.experimental import pallas as pl
from jax.experimental.pallas import tpu as pltpu
from jax.sharding import Mesh, PartitionSpec as P

HEAD_DIM = 128
AXES = ("yl", "x", "core", "yh", "z")
SIZES = (2, 4, 2, 2, 8)
FRAME = AXES[:3]
TOK = AXES[3:]
FRAMES = 16
PATCHES = 128
CUT_A, CUT_B = 48, 96
CUTS = ((0, CUT_A), (CUT_A, CUT_B), (CUT_B, PATCHES))
STEP = 4
FAR = (4,)
NEAR = ((3, 5), (2, 6), (1, 7, 0))
CUT_FLOPS = 3 * 10**10
WIDTH = 4096
COLS = 3 * HEAD_DIM
ROWS = FRAMES * PATCHES
GROUP = 16
CHUNK = WIDTH // 8
SHARE = jax.ShapeDtypeStruct((2, 3, CHUNK // 2, HEAD_DIM), jnp.bfloat16)

SAME_CORE = ((0, 0), (0, 1), (0, -1), (1, 0), (0, 2), (1, 1), (1, -1), (1, 2))
SLOTS = [(dy, dx, dc) for dy, dx in SAME_CORE for dc in (0, 1)]


def device(yl, x, core, yh, z):
    place = 0
    for value, size in zip((yl, x, core, yh, z), SIZES):
        place = place * size + value % size
    return place


def worker_moves():
    pairs = []
    for yl, x, core, yh, z in np.ndindex(*SIZES):
        owner = device(yl ^ (z % 2), x + z // 2, yh, core, 2 * x + yl)
        pairs.append((owner, device(yl, x, core, yh, z)))
    return pairs


def cross_moves(by):
    return [(yh * 8 + z, (1 - yh) * 8 + (z + by) % 8) for yh in range(2) for z in range(8)]


def plane_moves():
    pairs = []
    for yl, x, core, yh, z in np.ndindex(*SIZES):
        target = device(yl ^ (z % 2), x + z // 2, yh, core, z)
        pairs.append((device(yl, x, core, yh, z), target))
    return pairs


def line_moves():
    pairs = []
    for yl, x, core, yh, z in np.ndindex(*SIZES):
        target = device(yl, x, core, yh, 2 * ((x - z // 2) % 4) + (yl ^ (z % 2)))
        pairs.append((device(yl, x, core, yh, z), target))
    return pairs


def shift(value, axis, by):
    count = SIZES[AXES.index(axis)]
    return lax.ppermute(value, axis, [(i, (i + by) % count) for i in range(count)])


def after(values, *others):
    return lax.optimization_barrier((values, *others))[0]


def cut_kernel(*refs):
    sems = refs[-1]
    copies = []
    for index, (first, last) in enumerate(CUTS):
        source, target = refs[index], refs[3 + index]
        copies.append(
            pltpu.make_async_copy(source.at[pl.ds(first, last - first)], target, sems.at[index])
        )
        copies[-1].start()
    for copy in copies:
        copy.wait()


def cut(*buffers):
    hbm = pl.BlockSpec(memory_space=pltpu.HBM)
    return pl.pallas_call(
        cut_kernel,
        out_shape=[
            jax.ShapeDtypeStruct((last - first, WIDTH), jnp.bfloat16) for first, last in CUTS
        ],
        in_specs=[hbm] * 3,
        out_specs=[pl.BlockSpec(memory_space=pltpu.VMEM)] * 3,
        scratch_shapes=[pltpu.SemaphoreType.DMA((3,))],
        cost_estimate=pl.CostEstimate(flops=CUT_FLOPS, bytes_accessed=0, transcendentals=0),
    )(*buffers)


def gather_frames(own, early, middle, late):
    twin = lambda values: [shift(value, "core", 1) for value in values]
    first = [shift(own, "x", 1), shift(own, "x", -1), shift(own, "yl", 1)]
    own_twin = shift(own, "core", 1)
    left, right, other = after(first, *early)
    second = [shift(other, "x", 1), shift(right, "x", -1), shift(right, "yl", 1)]
    first_twins = twin([left, right, other])
    other_left, far, other_right = after(second, *middle)
    cuts = cut(other_left, other_right, far)
    third = [shift(cuts[0], "x", 1), shift(cuts[1], "x", -1), shift(cuts[2], "yl", 1)]
    second_twins = twin([other_left, far, other_right])
    third = after(third, *late)
    return (
        [own, own_twin, left, right, other, *first_twins],
        [other_left, far, other_right, *second_twins],
        [*third, *twin(third)],
    )


FIRST = [[(slot, 0, PATCHES)] for slot in (0, 1, 4, 2, 6, 5, 3, 7)]
SECOND = [[(slot, 0, PATCHES)] for slot in (12, 8, 10, 13, 9, 11)]
THIRD = [
    [(14 + core, first, last - first)]
    for core in (0, 1)
    for first, last in CUTS
]


def parts_of(places):
    out = []
    for buffer, parts in enumerate(places):
        row = 0
        for slot, first, rows in parts:
            out.append((buffer, row // GROUP, slot, first // GROUP, rows // GROUP))
            row += rows
    return out


PARTS = parts_of(FIRST + SECOND + THIRD)


def tables():
    out = np.zeros((256, 48), np.int32)
    for yl, x, core, yh, z in np.ndindex(*SIZES):
        row = out[device(yl, x, core, yh, z)]
        for slot, (dy, dx, dc) in enumerate(SLOTS):
            row[slot] = (core ^ dc) * 8 + (x + dx) % 4 * 2 + (yl ^ dy)
            row[24 + slot] = ((yl ^ dy) * 4 + (x + dx) % 4) * 2 + (core ^ dc)
        for k in range(8):
            at = (z + k) % 8
            row[16 + k] = (yl ^ (at % 2)) * 4 + (x + at // 2) % 4
        row[40] = (x - z // 2) % 4 * 2 + (yl ^ (z % 2))
    return out


def visible(ids):
    frame = jnp.repeat(ids, GROUP)
    patch = jnp.tile(jnp.arange(GROUP, dtype=jnp.int32), FRAMES)
    allowed = (frame[None, :] <= frame[:, None]) & (patch[None, :] == patch[:, None])
    return allowed.astype(jnp.float32)


VMEM = pl.BlockSpec(memory_space=pltpu.VMEM)
SMEM = pl.BlockSpec(memory_space=pltpu.SMEM)
HBM = pl.BlockSpec(memory_space=pltpu.HBM)


def take_kernel(start, w_ref, out, sem):
    copies = []
    for j in range(3):
        rows = pl.ds(pl.multiple_of(start[0] * CHUNK, CHUNK), CHUNK)
        columns = pl.ds(j * HEAD_DIM, HEAD_DIM)
        copies.append(pltpu.make_async_copy(w_ref.at[j, rows], out.at[:, columns], sem.at[j]))
        copies[-1].start()
    for copy in copies:
        copy.wait()


def take_rows(start, w):
    return pl.pallas_call(
        take_kernel,
        out_shape=jax.ShapeDtypeStruct((CHUNK, COLS), jnp.bfloat16),
        in_specs=[SMEM, HBM],
        out_specs=VMEM,
        scratch_shapes=[pltpu.SemaphoreType.DMA((3,))],
    )(start, w)


def attend(proj, grads, mask, turned):
    factor = 1.0 / math.sqrt(HEAD_DIM)
    size = FRAMES * GROUP

    def body(step, carry):
        part = proj[step].reshape(size, COLS)
        query, key, value = (part[:, j * HEAD_DIM : (j + 1) * HEAD_DIM] for j in range(3))
        grad = grads[step].reshape(size, HEAD_DIM)
        across = (((1,), (1,)), ((), ()))
        down = (((0,), (0,)), ((), ()))
        dot = functools.partial(lax.dot_general, preferred_element_type=jnp.float32)
        scores = dot(query, key, across) * factor
        scores = jnp.where(mask[...] > 0.5, scores, -1e30)
        exponent = jnp.exp(scores - jnp.max(scores, axis=-1, keepdims=True))
        probs = exponent / jnp.sum(exponent, axis=-1, keepdims=True)
        grad_probs = dot(grad, value, across)
        row_dot = jnp.sum(grad_probs * probs, axis=-1, keepdims=True)
        grad_scores = (probs * (grad_probs - row_dot)).astype(jnp.bfloat16)
        probs_b = probs.astype(jnp.bfloat16)
        grad_query = jnp.dot(grad_scores, key, preferred_element_type=jnp.float32) * factor
        grad_key = dot(grad_scores, query, down) * factor
        grad_value = dot(probs_b, grad, down)
        columns = pl.ds(pl.multiple_of(step * size, size), size)
        for j, result in enumerate((grad_query, grad_key, grad_value)):
            turned[j * HEAD_DIM : (j + 1) * HEAD_DIM, columns] = result.T.astype(jnp.bfloat16)
        return carry

    lax.fori_loop(0, PATCHES // GROUP, body, 0, unroll=4)


def share_kernel(count, order, mask, w_ref, g_ref, *refs):
    buffers, turned_out, out = refs[:count], refs[count], refs[count + 1 : count + 1 + len(FAR)]
    tokens, proj, grads, turned, w, w_sem, x_sem, g_sem = refs[count + 1 + len(FAR) :]
    arrivals = [[] for _ in range(FRAMES)]
    for index, (buffer, at, slot, first, groups) in enumerate(PARTS):
        arrivals[slot].append(
            pltpu.make_async_copy(
                buffers[buffer].at[pl.ds(at, groups)],
                tokens.at[pl.ds(first, groups), slot],
                x_sem.at[index],
            )
        )
    cotangents = []
    for slot in range(FRAMES):
        cotangents.append(
            pltpu.make_async_copy(g_ref.at[order[slot]], grads.at[:, slot], g_sem.at[slot])
        )
    weights = pltpu.make_async_copy(w_ref, w, w_sem.at[0])

    def step_copies(step):
        return [copy for slot in range(STEP * step, STEP * step + STEP) for copy in arrivals[slot]]

    weights.start()
    for copy in step_copies(0):
        copy.start()
    weights.wait()
    steps = FRAMES // STEP
    for step in range(steps):
        for copy in step_copies(step):
            copy.wait()
        for copy in step_copies(step + 1) if step + 1 < steps else cotangents:
            copy.start()
        slots = slice(STEP * step, STEP * step + STEP)
        rows = tokens[:, slots].reshape(STEP * PATCHES, WIDTH)
        result = jnp.dot(rows, w[...], preferred_element_type=jnp.float32)
        proj[:, slots] = result.astype(jnp.bfloat16).reshape(-1, STEP, GROUP, COLS)
    for copy in cotangents:
        copy.wait()
    attend(proj, grads, mask, turned)
    store = pltpu.make_async_copy(turned, turned_out, w_sem.at[1])
    store.start()
    for index, ahead in enumerate(FAR):
        columns = pl.ds(pl.multiple_of(order[16 + ahead] * CHUNK, CHUNK), CHUNK)
        rows = tokens[:, :, :, columns].reshape(ROWS, CHUNK)
        weigh(turned, rows, out[index])
    store.wait()


def weigh(turned, rows, out):
    value = jnp.dot(turned[...], rows, preferred_element_type=jnp.float32)
    for half in range(2):
        rows = slice(half * CHUNK // 2, (half + 1) * CHUNK // 2)
        for j in range(3):
            part = value[j * HEAD_DIM : (j + 1) * HEAD_DIM, rows]
            out[half, j] = part.T.astype(jnp.bfloat16)


def near_kernel(count, near, order, turned_ref, *refs):
    buffers, out = refs[:count], refs[count : count + len(near)]
    tokens, turned, t_sem, x_sem = refs[count + len(near) :]
    load = pltpu.make_async_copy(turned_ref, turned, t_sem.at[0])
    load.start()
    copies = []
    for index, ahead in enumerate(near):
        columns = pl.ds(pl.multiple_of(order[16 + ahead] * CHUNK, CHUNK), CHUNK)
        copies.append([])
        for part, (buffer, at, slot, first, groups) in enumerate(PARTS):
            copies[-1].append(
                pltpu.make_async_copy(
                    buffers[buffer].at[pl.ds(at, groups), :, columns],
                    tokens.at[index, pl.ds(first, groups), slot],
                    x_sem.at[index, part],
                )
            )
    for copy in copies[0] + copies[1]:
        copy.start()
    load.wait()
    for index in range(len(near)):
        for copy in copies[index]:
            copy.wait()
        if index + 2 < len(near):
            for copy in copies[index + 2]:
                copy.start()
        weigh(turned, tokens[index].reshape(ROWS, CHUNK), out[index])


def near_shares(order, turned, buffers, near):
    count = len(buffers)
    return pl.pallas_call(
        functools.partial(near_kernel, count, near),
        out_shape=[SHARE] * len(near),
        in_specs=[SMEM] + [HBM] * (1 + count),
        out_specs=[VMEM] * len(near),
        scratch_shapes=[
            pltpu.VMEM((len(near), PATCHES // GROUP, FRAMES, GROUP, CHUNK), jnp.bfloat16),
            pltpu.VMEM((COLS, ROWS), jnp.bfloat16),
            pltpu.SemaphoreType.DMA((1,)),
            pltpu.SemaphoreType.DMA((len(near), len(PARTS))),
        ],
        compiler_params=pltpu.CompilerParams(vmem_limit_bytes=50 * 2**20),
        cost_estimate=pl.CostEstimate(
            flops=2 * ROWS * len(near) * CHUNK * COLS,
            bytes_accessed=2 * ROWS * len(near) * CHUNK,
            transcendentals=0,
        ),
    )(order, turned, *buffers)


def far_shares(order, mask, w, g, buffers):
    count = len(buffers)
    groups = PATCHES // GROUP
    return pl.pallas_call(
        functools.partial(share_kernel, count),
        out_shape=[jax.ShapeDtypeStruct((COLS, ROWS), jnp.bfloat16)] + [SHARE] * len(FAR),
        in_specs=[SMEM, VMEM] + [HBM] * (2 + count),
        out_specs=[HBM] + [VMEM] * len(FAR),
        scratch_shapes=[
            pltpu.VMEM((groups, FRAMES, GROUP, WIDTH), jnp.bfloat16),
            pltpu.VMEM((groups, FRAMES, GROUP, COLS), jnp.bfloat16),
            pltpu.VMEM((groups, FRAMES, GROUP, HEAD_DIM), jnp.bfloat16),
            pltpu.VMEM((COLS, ROWS), jnp.bfloat16),
            pltpu.VMEM((WIDTH, COLS), jnp.bfloat16),
            pltpu.SemaphoreType.DMA((2,)),
            pltpu.SemaphoreType.DMA((len(PARTS),)),
            pltpu.SemaphoreType.DMA((FRAMES,)),
        ],
        compiler_params=pltpu.CompilerParams(vmem_limit_bytes=49 * 2**20),
        cost_estimate=pl.CostEstimate(
            flops=2 * ROWS * WIDTH * COLS, bytes_accessed=2 * ROWS * WIDTH, transcendentals=0
        ),
    )(order, mask, w, g, *buffers)


def add(*parts):
    return sum(part.astype(jnp.float32) for part in parts).astype(jnp.bfloat16)


def local(inputs, grad_attn, w_qkv):
    table = jnp.asarray(tables())[lax.axis_index(AXES)]
    rows_w = take_rows(table[40:41], w_qkv.transpose(1, 0, 2))
    rows_w = lax.ppermute(rows_w, AXES, worker_moves())
    w = lax.all_gather(rows_w, "z", axis=0, tiled=True)
    exchange = lambda value, axes: lax.all_to_all(
        value, axes, split_axis=0, concat_axis=0, tiled=True
    )
    heads_g = exchange(after(grad_attn[0], rows_w).reshape(FRAMES, PATCHES, HEAD_DIM), TOK)
    frames_g = exchange(heads_g, ("core", "x", "yl"))
    steps = gather_frames(inputs[0], (rows_w,), (heads_g,), (frames_g,))
    g = frames_g.reshape(FRAMES, PATCHES // GROUP, GROUP, HEAD_DIM)
    first, second, third = (
        [buffer.reshape(-1, GROUP, WIDTH) for buffer in buffers] for buffers in steps
    )
    order, buffers = table[:24], first + second + third
    turned, far = far_shares(order, visible(table[24:40]), w, g, buffers)
    beside = lax.optimization_barrier
    shares = lambda near: near_shares(order, turned, buffers, near)
    up, down, near = beside((shift(far[0], "z", 1), shift(far[1], "z", -1), shares(NEAR[0])))
    up = jnp.stack((add(up, near[0][0]), near[0][1]))
    down = jnp.stack((near[1][0], add(down, near[1][1])))
    for step in NEAR[1:]:
        up, down, near = beside((shift(up, "z", 1), shift(down, "z", -1), shares(step)))
        up, down = add(up, near[0]), add(down, near[1])
    yh = lax.axis_index("yh")
    half = lambda value, flip: lax.dynamic_index_in_dim(value, (yh + flip) % 2, 0, keepdims=False)
    parts = [
        half(near[2], 0),
        shift(half(near[2], 1), "yh", 1),
        shift(half(up, 0), "z", 1),
        shift(half(down, 0), "z", -1),
        lax.ppermute(half(up, 1), TOK, cross_moves(1)),
        lax.ppermute(half(down, 1), TOK, cross_moves(-1)),
    ]
    mine = lax.ppermute(add(*parts), AXES, plane_moves())
    return lax.ppermute(mine, AXES, line_moves()).transpose(1, 0, 2)


def solution(mesh):
    fine = Mesh(mesh.devices.reshape(SIZES), AXES)
    in_specs = (P(FRAME, TOK, None), P(FRAME, None, TOK), P(None, None, TOK))
    out_specs = P(FRAME, None, TOK)
    return jax.shard_map(local, mesh=fine, in_specs=in_specs, out_specs=out_specs, check_vma=False)
```

```python
import functools
import math

import jax
import jax.numpy as jnp
import numpy as np
from jax import lax
from jax.experimental import pallas as pl
from jax.experimental.pallas import tpu as pltpu
from jax.sharding import Mesh, PartitionSpec as P

HEAD_DIM = 128
AXES = ("yl", "x", "core", "yh", "z")
SIZES = (2, 4, 2, 2, 8)
FRAME = AXES[:3]
TOK = AXES[3:]
FRAMES = 16
PATCHES = 128
CUT_A, CUT_B = 48, 96
CUTS = ((0, CUT_A), (CUT_A, CUT_B), (CUT_B, PATCHES))
STEP = 4
FAR = (4,)
NEAR = ((3, 5), (2, 6), (1, 7, 0))
CUT_FLOPS = 3 * 10**10
WIDTH = 4096
COLS = 3 * HEAD_DIM
ROWS = FRAMES * PATCHES
GROUP = 16
CHUNK = WIDTH // 8
SHARE = jax.ShapeDtypeStruct((2, 3, CHUNK // 2, HEAD_DIM), jnp.bfloat16)
HALF_SHARE = jax.ShapeDtypeStruct((3, CHUNK // 2, HEAD_DIM), jnp.bfloat16)

SAME_CORE = ((0, 0), (0, 1), (0, -1), (1, 0), (0, 2), (1, 1), (1, -1), (1, 2))
SLOTS = [(dy, dx, dc) for dy, dx in SAME_CORE for dc in (0, 1)]


def device(yl, x, core, yh, z):
    place = 0
    for value, size in zip((yl, x, core, yh, z), SIZES):
        place = place * size + value % size
    return place


def worker_moves():
    pairs = []
    for yl, x, core, yh, z in np.ndindex(*SIZES):
        owner = device(yl ^ (z % 2), x + z // 2, yh, core, 2 * x + yl)
        pairs.append((owner, device(yl, x, core, yh, z)))
    return pairs


def plane_moves(flip):
    pairs = []
    for yl, x, core, yh, z in np.ndindex(*SIZES):
        target = device(yl ^ (z % 2), x + z // 2, yh ^ flip, core, z)
        pairs.append((device(yl, x, core, yh, z), target))
    return pairs


def line_moves():
    pairs = []
    for yl, x, core, yh, z in np.ndindex(*SIZES):
        target = device(yl, x, core, yh, 2 * ((x - z // 2) % 4) + (yl ^ (z % 2)))
        pairs.append((device(yl, x, core, yh, z), target))
    return pairs


def shift(value, axis, by):
    count = SIZES[AXES.index(axis)]
    return lax.ppermute(value, axis, [(i, (i + by) % count) for i in range(count)])


def after(values, *others):
    return lax.optimization_barrier((values, *others))[0]


def cut_kernel(*refs):
    sems = refs[-1]
    copies = []
    for index, (first, last) in enumerate(CUTS):
        source, target = refs[index], refs[3 + index]
        copies.append(
            pltpu.make_async_copy(source.at[pl.ds(first, last - first)], target, sems.at[index])
        )
        copies[-1].start()
    for copy in copies:
        copy.wait()


def cut(*buffers):
    hbm = pl.BlockSpec(memory_space=pltpu.HBM)
    return pl.pallas_call(
        cut_kernel,
        out_shape=[
            jax.ShapeDtypeStruct((last - first, WIDTH), jnp.bfloat16) for first, last in CUTS
        ],
        in_specs=[hbm] * 3,
        out_specs=[pl.BlockSpec(memory_space=pltpu.VMEM)] * 3,
        scratch_shapes=[pltpu.SemaphoreType.DMA((3,))],
        cost_estimate=pl.CostEstimate(flops=CUT_FLOPS, bytes_accessed=0, transcendentals=0),
    )(*buffers)


def gather_frames(own, early, middle, late):
    twin = lambda values: [shift(value, "core", 1) for value in values]
    first = [shift(own, "x", 1), shift(own, "x", -1), shift(own, "yl", 1)]
    own_twin = shift(own, "core", 1)
    left, right, other = after(first, *early)
    second = [shift(other, "x", 1), shift(right, "x", -1), shift(right, "yl", 1)]
    first_twins = twin([left, right, other])
    other_left, far, other_right = after(second, *middle)
    cuts = cut(other_left, other_right, far)
    third = [shift(cuts[0], "x", 1), shift(cuts[1], "x", -1), shift(cuts[2], "yl", 1)]
    second_twins = twin([other_left, far, other_right])
    third = after(third, *late)
    return (
        [own, own_twin, left, right, other, *first_twins],
        [other_left, far, other_right, *second_twins],
        [*third, *twin(third)],
    )


FIRST = [[(slot, 0, PATCHES)] for slot in (0, 1, 4, 2, 6, 5, 3, 7)]
SECOND = [[(slot, 0, PATCHES)] for slot in (12, 8, 10, 13, 9, 11)]
THIRD = [
    [(14 + core, first, last - first)]
    for core in (0, 1)
    for first, last in CUTS
]


def parts_of(places):
    out = []
    for buffer, parts in enumerate(places):
        row = 0
        for slot, first, rows in parts:
            out.append((buffer, row // GROUP, slot, first // GROUP, rows // GROUP))
            row += rows
    return out


PARTS = parts_of(FIRST + SECOND + THIRD)


def tables():
    out = np.zeros((256, 48), np.int32)
    for yl, x, core, yh, z in np.ndindex(*SIZES):
        row = out[device(yl, x, core, yh, z)]
        for slot, (dy, dx, dc) in enumerate(SLOTS):
            row[slot] = (core ^ dc) * 8 + (x + dx) % 4 * 2 + (yl ^ dy)
            row[24 + slot] = ((yl ^ dy) * 4 + (x + dx) % 4) * 2 + (core ^ dc)
        for k in range(8):
            at = (z + k) % 8
            row[16 + k] = (yl ^ (at % 2)) * 4 + (x + at // 2) % 4
        row[40] = (x - z // 2) % 4 * 2 + (yl ^ (z % 2))
    return out


def visible(ids):
    frame = jnp.repeat(ids, GROUP)
    patch = jnp.tile(jnp.arange(GROUP, dtype=jnp.int32), FRAMES)
    allowed = (frame[None, :] <= frame[:, None]) & (patch[None, :] == patch[:, None])
    return allowed.astype(jnp.float32)


VMEM = pl.BlockSpec(memory_space=pltpu.VMEM)
SMEM = pl.BlockSpec(memory_space=pltpu.SMEM)
HBM = pl.BlockSpec(memory_space=pltpu.HBM)


def take_kernel(start, w_ref, out, sem):
    copies = []
    for j in range(3):
        rows = pl.ds(pl.multiple_of(start[0] * CHUNK, CHUNK), CHUNK)
        columns = pl.ds(j * HEAD_DIM, HEAD_DIM)
        copies.append(pltpu.make_async_copy(w_ref.at[j, rows], out.at[:, columns], sem.at[j]))
        copies[-1].start()
    for copy in copies:
        copy.wait()


def take_rows(start, w):
    return pl.pallas_call(
        take_kernel,
        out_shape=jax.ShapeDtypeStruct((CHUNK, COLS), jnp.bfloat16),
        in_specs=[SMEM, HBM],
        out_specs=VMEM,
        scratch_shapes=[pltpu.SemaphoreType.DMA((3,))],
    )(start, w)


def attend(proj, grads, mask, turned):
    factor = 1.0 / math.sqrt(HEAD_DIM)
    size = FRAMES * GROUP

    def body(step, carry):
        part = proj[step].reshape(size, COLS)
        query, key, value = (part[:, j * HEAD_DIM : (j + 1) * HEAD_DIM] for j in range(3))
        grad = grads[step].reshape(size, HEAD_DIM)
        across = (((1,), (1,)), ((), ()))
        down = (((0,), (0,)), ((), ()))
        dot = functools.partial(lax.dot_general, preferred_element_type=jnp.float32)
        scores = dot(query, key, across) * factor
        scores = jnp.where(mask[...] > 0.5, scores, -1e30)
        exponent = jnp.exp(scores - jnp.max(scores, axis=-1, keepdims=True))
        probs = exponent / jnp.sum(exponent, axis=-1, keepdims=True)
        grad_probs = dot(grad, value, across)
        row_dot = jnp.sum(grad_probs * probs, axis=-1, keepdims=True)
        grad_scores = (probs * (grad_probs - row_dot)).astype(jnp.bfloat16)
        probs_b = probs.astype(jnp.bfloat16)
        grad_query = jnp.dot(grad_scores, key, preferred_element_type=jnp.float32) * factor
        grad_key = dot(grad_scores, query, down) * factor
        grad_value = dot(probs_b, grad, down)
        columns = pl.ds(pl.multiple_of(step * size, size), size)
        for j, result in enumerate((grad_query, grad_key, grad_value)):
            turned[j * HEAD_DIM : (j + 1) * HEAD_DIM, columns] = result.T.astype(jnp.bfloat16)
        return carry

    lax.fori_loop(0, PATCHES // GROUP, body, 0, unroll=4)


def share_kernel(count, order, mask, w_ref, g_ref, *refs):
    buffers, turned_out, out = refs[:count], refs[count], refs[count + 1 : count + 3]
    tokens, proj, grads, turned, w, w_sem, x_sem, g_sem = refs[count + 3 :]
    arrivals = [[] for _ in range(FRAMES)]
    for index, (buffer, at, slot, first, groups) in enumerate(PARTS):
        arrivals[slot].append(
            pltpu.make_async_copy(
                buffers[buffer].at[pl.ds(at, groups)],
                tokens.at[pl.ds(first, groups), slot],
                x_sem.at[index],
            )
        )
    cotangents = []
    for slot in range(FRAMES):
        cotangents.append(
            pltpu.make_async_copy(g_ref.at[order[slot]], grads.at[:, slot], g_sem.at[slot])
        )
    weights = pltpu.make_async_copy(w_ref, w, w_sem.at[0])

    def step_copies(step):
        return [copy for slot in range(STEP * step, STEP * step + STEP) for copy in arrivals[slot]]

    weights.start()
    for copy in step_copies(0):
        copy.start()
    weights.wait()
    steps = FRAMES // STEP
    for step in range(steps):
        for copy in step_copies(step):
            copy.wait()
        for copy in step_copies(step + 1) if step + 1 < steps else cotangents:
            copy.start()
        slots = slice(STEP * step, STEP * step + STEP)
        rows = tokens[:, slots].reshape(STEP * PATCHES, WIDTH)
        result = jnp.dot(rows, w[...], preferred_element_type=jnp.float32)
        proj[:, slots] = result.astype(jnp.bfloat16).reshape(-1, STEP, GROUP, COLS)
    for copy in cotangents:
        copy.wait()
    attend(proj, grads, mask, turned)
    store = pltpu.make_async_copy(turned, turned_out, w_sem.at[1])
    store.start()
    for ahead in FAR:
        columns = pl.ds(pl.multiple_of(order[16 + ahead] * CHUNK, CHUNK), CHUNK)
        rows = tokens[:, :, :, columns].reshape(ROWS, CHUNK)
        weigh(turned, rows, *out)
    store.wait()


def weigh(turned, rows, *out):
    value = jnp.dot(turned[...], rows, preferred_element_type=jnp.float32)
    for half in range(2):
        rows = slice(half * CHUNK // 2, (half + 1) * CHUNK // 2)
        for j in range(3):
            part = value[j * HEAD_DIM : (j + 1) * HEAD_DIM, rows]
            if len(out) == 2:
                out[half][j] = part.T.astype(jnp.bfloat16)
            else:
                out[0][half, j] = part.T.astype(jnp.bfloat16)


def near_kernel(count, near, order, turned_ref, *refs):
    buffers, out = refs[:count], refs[count : count + len(near)]
    tokens, turned, t_sem, x_sem = refs[count + len(near) :]
    load = pltpu.make_async_copy(turned_ref, turned, t_sem.at[0])
    load.start()
    copies = []
    for index, ahead in enumerate(near):
        columns = pl.ds(pl.multiple_of(order[16 + ahead] * CHUNK, CHUNK), CHUNK)
        copies.append([])
        for part, (buffer, at, slot, first, groups) in enumerate(PARTS):
            copies[-1].append(
                pltpu.make_async_copy(
                    buffers[buffer].at[pl.ds(at, groups), :, columns],
                    tokens.at[index, pl.ds(first, groups), slot],
                    x_sem.at[index, part],
                )
            )
    for copy in copies[0] + copies[1]:
        copy.start()
    load.wait()
    for index in range(len(near)):
        for copy in copies[index]:
            copy.wait()
        if index + 2 < len(near):
            for copy in copies[index + 2]:
                copy.start()
        weigh(turned, tokens[index].reshape(ROWS, CHUNK), out[index])


def near_shares(order, turned, buffers, near):
    count = len(buffers)
    return pl.pallas_call(
        functools.partial(near_kernel, count, near),
        out_shape=[SHARE] * len(near),
        in_specs=[SMEM] + [HBM] * (1 + count),
        out_specs=[VMEM] * len(near),
        scratch_shapes=[
            pltpu.VMEM((len(near), PATCHES // GROUP, FRAMES, GROUP, CHUNK), jnp.bfloat16),
            pltpu.VMEM((COLS, ROWS), jnp.bfloat16),
            pltpu.SemaphoreType.DMA((1,)),
            pltpu.SemaphoreType.DMA((len(near), len(PARTS))),
        ],
        compiler_params=pltpu.CompilerParams(vmem_limit_bytes=48 * 2**20),
        cost_estimate=pl.CostEstimate(
            flops=2 * ROWS * len(near) * CHUNK * COLS,
            bytes_accessed=2 * ROWS * len(near) * CHUNK,
            transcendentals=0,
        ),
    )(order, turned, *buffers)


def far_shares(order, mask, w, g, buffers):
    count = len(buffers)
    groups = PATCHES // GROUP
    return pl.pallas_call(
        functools.partial(share_kernel, count),
        out_shape=[jax.ShapeDtypeStruct((COLS, ROWS), jnp.bfloat16)] + [HALF_SHARE] * 2,
        in_specs=[SMEM, VMEM] + [HBM] * (2 + count),
        out_specs=[HBM] + [VMEM] * 2,
        scratch_shapes=[
            pltpu.VMEM((groups, FRAMES, GROUP, WIDTH), jnp.bfloat16),
            pltpu.VMEM((groups, FRAMES, GROUP, COLS), jnp.bfloat16),
            pltpu.VMEM((groups, FRAMES, GROUP, HEAD_DIM), jnp.bfloat16),
            pltpu.VMEM((COLS, ROWS), jnp.bfloat16),
            pltpu.VMEM((WIDTH, COLS), jnp.bfloat16),
            pltpu.SemaphoreType.DMA((2,)),
            pltpu.SemaphoreType.DMA((len(PARTS),)),
            pltpu.SemaphoreType.DMA((FRAMES,)),
        ],
        compiler_params=pltpu.CompilerParams(vmem_limit_bytes=48 * 2**20),
        cost_estimate=pl.CostEstimate(
            flops=2 * ROWS * WIDTH * COLS, bytes_accessed=2 * ROWS * WIDTH, transcendentals=0
        ),
    )(order, mask, w, g, *buffers)


def add(*parts):
    return sum(part.astype(jnp.float32) for part in parts).astype(jnp.bfloat16)


def local(inputs, grad_attn, w_qkv):
    table = jnp.asarray(tables())[lax.axis_index(AXES)]
    rows_w = take_rows(table[40:41], w_qkv.transpose(1, 0, 2))
    rows_w = lax.ppermute(rows_w, AXES, worker_moves())
    w = lax.all_gather(rows_w, "z", axis=0, tiled=True)
    exchange = lambda value, axes: lax.all_to_all(
        value, axes, split_axis=0, concat_axis=0, tiled=True
    )
    heads_g = exchange(after(grad_attn[0], rows_w).reshape(FRAMES, PATCHES, HEAD_DIM), TOK)
    frames_g = exchange(heads_g, ("core", "x", "yl"))
    steps = gather_frames(inputs[0], (rows_w,), (heads_g,), (frames_g,))
    g = frames_g.reshape(FRAMES, PATCHES // GROUP, GROUP, HEAD_DIM)
    first, second, third = (
        [buffer.reshape(-1, GROUP, WIDTH) for buffer in buffers] for buffers in steps
    )
    order, buffers = table[:24], first + second + third
    turned, *far = far_shares(order, visible(table[24:40]), w, g, buffers)
    beside = lax.optimization_barrier
    shares = lambda near: near_shares(order, turned, buffers, near)
    up, down, near = beside((shift(far[0], "z", 1), shift(far[1], "z", -1), shares(NEAR[0])))
    up = jnp.stack((add(up, near[0][0]), near[0][1]))
    down = jnp.stack((near[1][0], add(down, near[1][1])))
    for step in NEAR[1:]:
        up, down, near = beside((shift(up, "z", 1), shift(down, "z", -1), shares(step)))
        up, down = add(up, near[0]), add(down, near[1])
    mine = add(shift(up, "z", 1), shift(down, "z", -1), near[2])
    yh = lax.axis_index("yh")
    total = None
    for flip in range(2):
        part = lax.dynamic_index_in_dim(mine, (yh + flip) % 2, 0, keepdims=False)
        part = lax.ppermute(part, AXES, plane_moves(flip)).astype(jnp.float32)
        total = part if total is None else total + part
    return lax.ppermute(total.astype(jnp.bfloat16), AXES, line_moves()).transpose(1, 0, 2)


def solution(mesh):
    fine = Mesh(mesh.devices.reshape(SIZES), AXES)
    in_specs = (P(FRAME, TOK, None), P(FRAME, None, TOK), P(None, None, TOK))
    out_specs = P(FRAME, None, TOK)
    return jax.shard_map(local, mesh=fine, in_specs=in_specs, out_specs=out_specs, check_vma=False)
```

```python
import functools
import math

import jax
import jax.numpy as jnp
import numpy as np
from jax import lax
from jax.experimental import pallas as pl
from jax.experimental.pallas import tpu as pltpu
from jax.sharding import Mesh, PartitionSpec as P

HEAD_DIM = 128
AXES = ("yl", "x", "core", "yh", "z")
SIZES = (2, 4, 2, 2, 8)
FRAME = AXES[:3]
TOK = AXES[3:]
FRAMES = 16
PATCHES = 128
CUT_A, CUT_B = 48, 96
CUTS = ((0, CUT_A), (CUT_A, CUT_B), (CUT_B, PATCHES))
STEP = 4
FAR = (4,)
NEAR = ((3, 5), (2, 6), (1, 7, 0))
CUT_FLOPS = 3 * 10**10
WIDTH = 4096
COLS = 3 * HEAD_DIM
ROWS = FRAMES * PATCHES
GROUP = 16
CHUNK = WIDTH // 8
SHARE = jax.ShapeDtypeStruct((2, 3, CHUNK // 2, HEAD_DIM), jnp.bfloat16)
HALF_SHARE = jax.ShapeDtypeStruct((3, CHUNK // 2, HEAD_DIM), jnp.bfloat16)

SAME_CORE = ((0, 0), (0, 1), (0, -1), (1, 0), (0, 2), (1, 1), (1, -1), (1, 2))
SLOTS = [(dy, dx, dc) for dy, dx in SAME_CORE for dc in (0, 1)]


def device(yl, x, core, yh, z):
    place = 0
    for value, size in zip((yl, x, core, yh, z), SIZES):
        place = place * size + value % size
    return place


def worker_moves():
    pairs = []
    for yl, x, core, yh, z in np.ndindex(*SIZES):
        owner = device(yl ^ (z % 2), x + z // 2, yh, core, 2 * x + yl)
        pairs.append((owner, device(yl, x, core, yh, z)))
    return pairs


def plane_moves(flip):
    pairs = []
    for yl, x, core, yh, z in np.ndindex(*SIZES):
        target = device(yl ^ (z % 2), x + z // 2, yh ^ flip, core, z)
        pairs.append((device(yl, x, core, yh, z), target))
    return pairs


def line_moves():
    pairs = []
    for yl, x, core, yh, z in np.ndindex(*SIZES):
        target = device(yl, x, core, yh, 2 * ((x - z // 2) % 4) + (yl ^ (z % 2)))
        pairs.append((device(yl, x, core, yh, z), target))
    return pairs


def shift(value, axis, by):
    count = SIZES[AXES.index(axis)]
    return lax.ppermute(value, axis, [(i, (i + by) % count) for i in range(count)])


def after(values, *others):
    return lax.optimization_barrier((values, *others))[0]


def cut_kernel(*refs):
    sems = refs[-1]
    copies = []
    for index, (first, last) in enumerate(CUTS):
        source, target = refs[index], refs[3 + index]
        copies.append(
            pltpu.make_async_copy(source.at[pl.ds(first, last - first)], target, sems.at[index])
        )
        copies[-1].start()
    for copy in copies:
        copy.wait()


def cut(*buffers):
    hbm = pl.BlockSpec(memory_space=pltpu.HBM)
    return pl.pallas_call(
        cut_kernel,
        out_shape=[
            jax.ShapeDtypeStruct((last - first, WIDTH), jnp.bfloat16) for first, last in CUTS
        ],
        in_specs=[hbm] * 3,
        out_specs=[pl.BlockSpec(memory_space=pltpu.VMEM)] * 3,
        scratch_shapes=[pltpu.SemaphoreType.DMA((3,))],
        cost_estimate=pl.CostEstimate(flops=CUT_FLOPS, bytes_accessed=0, transcendentals=0),
    )(*buffers)


def gather_frames(own, early, middle, late):
    twin = lambda values: [shift(value, "core", 1) for value in values]
    first = [shift(own, "x", 1), shift(own, "x", -1), shift(own, "yl", 1)]
    own_twin = shift(own, "core", 1)
    left, right, other = after(first, *early)
    second = [shift(other, "x", 1), shift(right, "x", -1), shift(right, "yl", 1)]
    first_twins = twin([left, right, other])
    other_left, far, other_right = after(second, *middle)
    cuts = cut(other_left, other_right, far)
    third = [shift(cuts[0], "x", 1), shift(cuts[1], "x", -1), shift(cuts[2], "yl", 1)]
    second_twins = twin([other_left, far, other_right])
    third = after(third, *late)
    return (
        [own, own_twin, left, right, other, *first_twins],
        [other_left, far, other_right, *second_twins],
        [*third, *twin(third)],
    )


FIRST = [[(slot, 0, PATCHES)] for slot in (0, 1, 4, 2, 6, 5, 3, 7)]
SECOND = [[(slot, 0, PATCHES)] for slot in (12, 8, 10, 13, 9, 11)]
THIRD = [
    [(14 + core, first, last - first)]
    for core in (0, 1)
    for first, last in CUTS
]


def parts_of(places):
    out = []
    for buffer, parts in enumerate(places):
        row = 0
        for slot, first, rows in parts:
            out.append((buffer, row // GROUP, slot, first // GROUP, rows // GROUP))
            row += rows
    return out


PARTS = parts_of(FIRST + SECOND + THIRD)


def tables():
    out = np.zeros((256, 48), np.int32)
    for yl, x, core, yh, z in np.ndindex(*SIZES):
        row = out[device(yl, x, core, yh, z)]
        for slot, (dy, dx, dc) in enumerate(SLOTS):
            row[slot] = (core ^ dc) * 8 + (x + dx) % 4 * 2 + (yl ^ dy)
            row[24 + slot] = ((yl ^ dy) * 4 + (x + dx) % 4) * 2 + (core ^ dc)
        for k in range(8):
            at = (z + k) % 8
            row[16 + k] = (yl ^ (at % 2)) * 4 + (x + at // 2) % 4
        row[40] = (x - z // 2) % 4 * 2 + (yl ^ (z % 2))
    return out


def visible(ids):
    frame = jnp.repeat(ids, GROUP)
    patch = jnp.tile(jnp.arange(GROUP, dtype=jnp.int32), FRAMES)
    allowed = (frame[None, :] <= frame[:, None]) & (patch[None, :] == patch[:, None])
    return allowed.astype(jnp.float32)


VMEM = pl.BlockSpec(memory_space=pltpu.VMEM)
SMEM = pl.BlockSpec(memory_space=pltpu.SMEM)
HBM = pl.BlockSpec(memory_space=pltpu.HBM)


def take_kernel(start, w_ref, out, sem):
    copies = []
    for j in range(3):
        rows = pl.ds(pl.multiple_of(start[0] * CHUNK, CHUNK), CHUNK)
        columns = pl.ds(j * HEAD_DIM, HEAD_DIM)
        copies.append(pltpu.make_async_copy(w_ref.at[j, rows], out.at[:, columns], sem.at[j]))
        copies[-1].start()
    for copy in copies:
        copy.wait()


def take_rows(start, w):
    return pl.pallas_call(
        take_kernel,
        out_shape=jax.ShapeDtypeStruct((CHUNK, COLS), jnp.bfloat16),
        in_specs=[SMEM, HBM],
        out_specs=VMEM,
        scratch_shapes=[pltpu.SemaphoreType.DMA((3,))],
    )(start, w)


def attend(proj, grads, mask, turned):
    factor = 1.0 / math.sqrt(HEAD_DIM)
    size = FRAMES * GROUP

    def body(step, carry):
        part = proj[step].reshape(size, COLS)
        query, key, value = (part[:, j * HEAD_DIM : (j + 1) * HEAD_DIM] for j in range(3))
        grad = grads[step].reshape(size, HEAD_DIM)
        across = (((1,), (1,)), ((), ()))
        down = (((0,), (0,)), ((), ()))
        dot = functools.partial(lax.dot_general, preferred_element_type=jnp.float32)
        scores = dot(query, key, across) * factor
        scores = jnp.where(mask[...] > 0.5, scores, -1e30)
        exponent = jnp.exp(scores - jnp.max(scores, axis=-1, keepdims=True))
        probs = exponent / jnp.sum(exponent, axis=-1, keepdims=True)
        grad_probs = dot(grad, value, across)
        row_dot = jnp.sum(grad_probs * probs, axis=-1, keepdims=True)
        grad_scores = (probs * (grad_probs - row_dot)).astype(jnp.bfloat16)
        probs_b = probs.astype(jnp.bfloat16)
        grad_query = jnp.dot(grad_scores, key, preferred_element_type=jnp.float32) * factor
        grad_key = dot(grad_scores, query, down) * factor
        grad_value = dot(probs_b, grad, down)
        columns = pl.ds(pl.multiple_of(step * size, size), size)
        for j, result in enumerate((grad_query, grad_key, grad_value)):
            turned[j * HEAD_DIM : (j + 1) * HEAD_DIM, columns] = result.T.astype(jnp.bfloat16)
        return carry

    lax.fori_loop(0, PATCHES // GROUP, body, 0, unroll=4)


def share_kernel(count, order, mask, w_ref, g_ref, *refs):
    buffers, turned_out, out = refs[:count], refs[count], refs[count + 1 : count + 3]
    tokens, proj, grads, turned, w, w_sem, x_sem, g_sem = refs[count + 3 :]
    arrivals = [[] for _ in range(FRAMES)]
    for index, (buffer, at, slot, first, groups) in enumerate(PARTS):
        arrivals[slot].append(
            pltpu.make_async_copy(
                buffers[buffer].at[pl.ds(at, groups)],
                tokens.at[pl.ds(first, groups), slot],
                x_sem.at[index],
            )
        )
    cotangents = []
    for slot in range(FRAMES):
        cotangents.append(
            pltpu.make_async_copy(g_ref.at[order[slot]], grads.at[:, slot], g_sem.at[slot])
        )
    weights = pltpu.make_async_copy(w_ref, w, w_sem.at[0])

    def step_copies(step):
        return [copy for slot in range(STEP * step, STEP * step + STEP) for copy in arrivals[slot]]

    weights.start()
    for copy in step_copies(0):
        copy.start()
    weights.wait()
    steps = FRAMES // STEP
    for step in range(steps):
        for copy in step_copies(step):
            copy.wait()
        for copy in step_copies(step + 1) if step + 1 < steps else cotangents:
            copy.start()
        slots = slice(STEP * step, STEP * step + STEP)
        rows = tokens[:, slots].reshape(STEP * PATCHES, WIDTH)
        result = jnp.dot(rows, w[...], preferred_element_type=jnp.float32)
        proj[:, slots] = result.astype(jnp.bfloat16).reshape(-1, STEP, GROUP, COLS)
    for copy in cotangents:
        copy.wait()
    attend(proj, grads, mask, turned)
    store = pltpu.make_async_copy(turned, turned_out, w_sem.at[1])
    store.start()
    for ahead in FAR:
        columns = pl.ds(pl.multiple_of(order[16 + ahead] * CHUNK, CHUNK), CHUNK)
        rows = tokens[:, :, :, columns].reshape(ROWS, CHUNK)
        weigh(turned, rows, *out)
    store.wait()


def weigh(turned, rows, *out):
    value = jnp.dot(turned[...], rows, preferred_element_type=jnp.float32)
    for half in range(2):
        rows = slice(half * CHUNK // 2, (half + 1) * CHUNK // 2)
        for j in range(3):
            part = value[j * HEAD_DIM : (j + 1) * HEAD_DIM, rows]
            if len(out) == 2:
                out[half][j] = part.T.astype(jnp.bfloat16)
            else:
                out[0][half, j] = part.T.astype(jnp.bfloat16)


def near_kernel(count, near, order, turned_ref, *refs):
    buffers, out = refs[:count], refs[count : count + len(near)]
    tokens, turned, t_sem, x_sem = refs[count + len(near) :]
    load = pltpu.make_async_copy(turned_ref, turned, t_sem.at[0])
    load.start()
    copies = []
    for index, ahead in enumerate(near):
        columns = pl.ds(pl.multiple_of(order[16 + ahead] * CHUNK, CHUNK), CHUNK)
        copies.append([])
        for part, (buffer, at, slot, first, groups) in enumerate(PARTS):
            copies[-1].append(
                pltpu.make_async_copy(
                    buffers[buffer].at[pl.ds(at, groups), :, columns],
                    tokens.at[index, pl.ds(first, groups), slot],
                    x_sem.at[index, part],
                )
            )
    for copy in copies[0] + copies[1]:
        copy.start()
    load.wait()
    for index in range(len(near)):
        for copy in copies[index]:
            copy.wait()
        if index + 2 < len(near):
            for copy in copies[index + 2]:
                copy.start()
        weigh(turned, tokens[index].reshape(ROWS, CHUNK), out[index])


def near_shares(order, turned, buffers, near):
    count = len(buffers)
    return pl.pallas_call(
        functools.partial(near_kernel, count, near),
        out_shape=[SHARE] * len(near),
        in_specs=[SMEM] + [HBM] * (1 + count),
        out_specs=[VMEM] * len(near),
        scratch_shapes=[
            pltpu.VMEM((len(near), PATCHES // GROUP, FRAMES, GROUP, CHUNK), jnp.bfloat16),
            pltpu.VMEM((COLS, ROWS), jnp.bfloat16),
            pltpu.SemaphoreType.DMA((1,)),
            pltpu.SemaphoreType.DMA((len(near), len(PARTS))),
        ],
        compiler_params=pltpu.CompilerParams(vmem_limit_bytes=48 * 2**20),
        cost_estimate=pl.CostEstimate(
            flops=2 * ROWS * len(near) * CHUNK * COLS,
            bytes_accessed=2 * ROWS * len(near) * CHUNK,
            transcendentals=0,
        ),
    )(order, turned, *buffers)


def far_shares(order, mask, w, g, buffers):
    count = len(buffers)
    groups = PATCHES // GROUP
    return pl.pallas_call(
        functools.partial(share_kernel, count),
        out_shape=[jax.ShapeDtypeStruct((COLS, ROWS), jnp.bfloat16)] + [HALF_SHARE] * 2,
        in_specs=[SMEM, VMEM] + [HBM] * (2 + count),
        out_specs=[HBM] + [VMEM] * 2,
        scratch_shapes=[
            pltpu.VMEM((groups, FRAMES, GROUP, WIDTH), jnp.bfloat16),
            pltpu.VMEM((groups, FRAMES, GROUP, COLS), jnp.bfloat16),
            pltpu.VMEM((groups, FRAMES, GROUP, HEAD_DIM), jnp.bfloat16),
            pltpu.VMEM((COLS, ROWS), jnp.bfloat16),
            pltpu.VMEM((WIDTH, COLS), jnp.bfloat16),
            pltpu.SemaphoreType.DMA((2,)),
            pltpu.SemaphoreType.DMA((len(PARTS),)),
            pltpu.SemaphoreType.DMA((FRAMES,)),
        ],
        compiler_params=pltpu.CompilerParams(vmem_limit_bytes=48 * 2**20),
        cost_estimate=pl.CostEstimate(
            flops=2 * ROWS * WIDTH * COLS, bytes_accessed=2 * ROWS * WIDTH, transcendentals=0
        ),
    )(order, mask, w, g, *buffers)


def add(*parts):
    return sum(part.astype(jnp.float32) for part in parts).astype(jnp.bfloat16)


def local(inputs, grad_attn, w_qkv):
    table = jnp.asarray(tables())[lax.axis_index(AXES)]
    rows_w = take_rows(table[40:41], w_qkv.transpose(1, 0, 2))
    rows_w = lax.ppermute(rows_w, AXES, worker_moves())
    w = lax.all_gather(rows_w, "z", axis=0, tiled=True)
    exchange = lambda value, axes: lax.all_to_all(
        value, axes, split_axis=0, concat_axis=0, tiled=True
    )
    heads_g = exchange(after(grad_attn[0], rows_w).reshape(FRAMES, PATCHES, HEAD_DIM), TOK)
    frames_g = exchange(heads_g, ("core", "x", "yl"))
    steps = gather_frames(inputs[0], (rows_w,), (heads_g,), (frames_g,))
    g = frames_g.reshape(FRAMES, PATCHES // GROUP, GROUP, HEAD_DIM)
    first, second, third = (
        [buffer.reshape(-1, GROUP, WIDTH) for buffer in buffers] for buffers in steps
    )
    order, buffers = table[:24], first + second + third
    turned, *far = far_shares(order, visible(table[24:40]), w, g, buffers)
    beside = lax.optimization_barrier
    shares = lambda near: near_shares(order, turned, buffers, near)
    up, down, near = beside((shift(far[0], "z", 1), shift(far[1], "z", -1), shares(NEAR[0])))
    up = jnp.stack((add(up, near[0][0]), near[0][1]))
    down = jnp.stack((near[1][0], add(down, near[1][1])))
    for step in NEAR[1:]:
        up, down, near = beside((shift(up, "z", 1), shift(down, "z", -1), shares(step)))
        up, down = add(up, near[0]), add(down, near[1])
    up, down = shift(up, "z", 1), shift(down, "z", -1)
    yh = lax.axis_index("yh")
    total = None
    for flip in range(2):
        half = lambda value: lax.dynamic_index_in_dim(value, (yh + flip) % 2, 0, keepdims=False)
        part = beside(add(half(up), half(down), half(near[2])))
        part = lax.ppermute(part, AXES, plane_moves(flip)).astype(jnp.float32)
        total = part if total is None else total + part
    return lax.ppermute(total.astype(jnp.bfloat16), AXES, line_moves()).transpose(1, 0, 2)


def solution(mesh):
    fine = Mesh(mesh.devices.reshape(SIZES), AXES)
    in_specs = (P(FRAME, TOK, None), P(FRAME, None, TOK), P(None, None, TOK))
    out_specs = P(FRAME, None, TOK)
    return jax.shard_map(local, mesh=fine, in_specs=in_specs, out_specs=out_specs, check_vma=False)
```
